256 devices in a mesh: terms: 64 (over x, z_lo, y, core), rows: 4 (over z_hi).
Axes of the slice: x: 4, y: 4, z: 8 (z_hi: 4, z_lo: 2; z = z_hi * 2 + z_lo), core: 2. Of those that a mesh axis runs over, the one named last changes fastest.
Arguments:
- amplitudes: float32 [768, 768], P('rows'), may hold values from -6 to 6
- left_terms: float32 [64, 768, 768], P('terms', 'rows'), may hold values from -0.02734375 to 0.02734375
- right_terms: float32 [64, 768, 768], P('terms'), may hold values from -0.21875 to 0.21875
- source_list: int32 [64, 4], replicated, may hold values from 0 to 63, as said below
- list_count: int32 [64], replicated, may hold values from 1 to 4
- weight_index: int32 [64, 4], replicated, may hold values from 0 to 7
- weight_table: float32 [8], replicated, may hold values from -4 to 4
Outputs:
- isometry: float32 [768, 768], P('rows')
- new_environment: float32 [64, 768, 768], P('terms', 'rows')
The draws below stay inside these ranges and needn't reach their ends.
Inputs may be any that keep to these rules, and one draw needn't show every extreme that they name: `source_list`: every block id appears in column 0 exactly once.
All inputs are finite; a program needn't handle non-finite values.
Results may differ from the reference program's by a relative error of at most 0.00016.
Values sent between devices are 32-bit elements; how exact they have to be, the bound alone decides.
A program may use at most 64 MiB of HBM per device.

```python
import math
import jax
import jax.numpy as jnp
from jax import lax

K = 768
FAN = 4
NCOEF = 8
SWEEPS = 3
TERMS = 64


def draw_source_list(key, part):
    first_key, other_key = jax.random.split(jax.random.fold_in(key, 11))
    leading = jax.random.permutation(first_key, TERMS).astype(jnp.int32)
    others = jax.random.randint(other_key, (TERMS, FAN - 1), 0, TERMS).astype(jnp.int32)
    return jnp.concatenate([leading[:, None], others], axis=1).astype(jnp.int32)


def draw_list_count(key, part):
    count_key, place_key = jax.random.split(jax.random.fold_in(key, 23))
    counts = jax.random.randint(count_key, (TERMS,), 1, FAN + 1).astype(jnp.int32)
    places = jax.random.permutation(place_key, TERMS)
    counts = counts.at[places[0]].set(FAN)
    counts = counts.at[places[1]].set(1)
    return counts.astype(jnp.int32)


def draw_weight_index(key, part):
    first_key, other_key = jax.random.split(jax.random.fold_in(key, 37))
    leading = (jax.random.permutation(first_key, TERMS) % NCOEF).astype(jnp.int32)
    others = jax.random.randint(other_key, (TERMS, FAN - 1), 0, NCOEF).astype(jnp.int32)
    return jnp.concatenate([leading[:, None], others], axis=1).astype(jnp.int32)


def block_levels(rng, extent, shards, smallest, largest):
    gain = 1.0
    for position, blocks in shards:
        steps = jax.random.uniform(jax.random.fold_in(jax.random.fold_in(rng, 6), position), (blocks,), jnp.float32, smallest / len(shards), largest / len(shards))
        gain = gain * jnp.repeat(jnp.exp(steps), extent[position] // blocks).reshape((-1,) + (1,) * (len(extent) - 1 - position))
    return gain


def centred(key, dims, scale, bound, cuts=(), held_as=jnp.bfloat16):
    result = jax.random.normal(key, dims, jnp.float32) * scale
    if len(cuts) > 0:
        result = block_levels(key, dims, cuts, -0.22, 0.18) * result
    return jnp.clip(result, min=-bound, max=bound).astype(held_as)


def setup_inputs(seed: int = 0) -> dict:
    keys = jax.random.split(jax.random.key(seed), 8)
    return {
        "amplitudes": centred(keys[0], (K, K), 1.0, 6.0, ((0, 4),), jnp.float32),
        "left_terms": centred(keys[1], (TERMS, K, K), (K * TERMS) ** -0.5, 0.02734375, ((0, 64), (1, 4)), jnp.float32),
        "right_terms": centred(keys[2], (TERMS, K, K), K ** -0.5, 0.21875, ((0, 64),), jnp.float32),
        "source_list": draw_source_list(jax.random.fold_in(keys[7], 71), 0),
        "list_count": draw_list_count(jax.random.fold_in(keys[7], 71), 0),
        "weight_index": draw_weight_index(jax.random.fold_in(keys[7], 71), 0),
        "weight_table": centred(keys[6], (NCOEF,), 1.0, 4.0, (), jnp.float32),
    }


HIGH = lax.Precision.HIGHEST
COEF_ONE = 3.4445
COEF_TWO = -4.775
COEF_THREE = 2.0315

def apply_terms(amplitudes, left_terms, right_terms):

    def accumulate(summed, pair):
        left_block, right_block = pair
        mapped = jnp.dot(left_block, amplitudes, precision=HIGH, preferred_element_type=jnp.float32)
        return (summed + jnp.dot(mapped, right_block, precision=HIGH, preferred_element_type=jnp.float32), None)
    summed, _ = lax.scan(accumulate, jnp.zeros(amplitudes.shape, jnp.float32), (left_terms, right_terms))
    return amplitudes - 0.3 * summed

def combination(source_list, list_count, weight_index, weight_table):
    in_use = (jnp.arange(FAN)[None, :] < list_count[:, None]).astype(jnp.float32)
    picked = (weight_index[:, :, None] == jnp.arange(NCOEF)[None, None, :]).astype(jnp.float32)
    weights = jnp.einsum('jcn,n->jc', picked, weight_table.astype(jnp.float32), precision=HIGH) * in_use
    matches = (source_list[:, :, None] == jnp.arange(TERMS)[None, None, :]).astype(jnp.float32)
    return jnp.einsum('jc,jcb->jb', weights, matches, precision=HIGH)

def reference(amplitudes, left_terms, right_terms, source_list, list_count, weight_index, weight_table):
    first = apply_terms(amplitudes, left_terms, right_terms)
    second = apply_terms(first, left_terms, right_terms)
    squares = jnp.sum(second * second)
    iterate = second / jnp.sqrt(squares)
    for repeat in range(SWEEPS):
        gram_matrix = jnp.dot(iterate.T, iterate, precision=HIGH, preferred_element_type=jnp.float32)
        once = jnp.dot(iterate, gram_matrix, precision=HIGH, preferred_element_type=jnp.float32)
        twice = jnp.dot(once, gram_matrix, precision=HIGH, preferred_element_type=jnp.float32)
        iterate = COEF_ONE * iterate + COEF_TWO * once + COEF_THREE * twice
    isometry = math.sqrt(K) * iterate
    mixing = combination(source_list, list_count, weight_index, weight_table)

    def one_block(weights):
        combined = jnp.einsum('b,bkl->kl', weights, left_terms, precision=HIGH)
        rotated = jnp.dot(combined, isometry, precision=HIGH, preferred_element_type=jnp.float32)
        return jnp.dot(isometry.T, rotated, precision=HIGH, preferred_element_type=jnp.float32)
    new_environment = lax.map(one_block, mixing)
    return (isometry, new_environment)
```

```python
import math

import jax
import jax.numpy as jnp
from jax import lax
from jax.experimental import pallas as pl
from jax.experimental.pallas import tpu as pltpu
from jax.sharding import PartitionSpec as P

K = 768
FAN = 4
SWEEPS = 3
SLAB = 192
OWNERS = 48
TR, TC = 8, 384
COEF_ONE = 3.4445
COEF_TWO = -4.775
COEF_THREE = 2.0315
MESH = pl.DeviceIdType.MESH
BF = jnp.bfloat16
F32 = jnp.float32


def halves(value):
    high = value.astype(BF)
    return high, (value - high.astype(F32)).astype(BF)


def split(src, high, low, rows, step):
    @pl.loop(0, rows // step)
    def _(i):
        at = pl.ds(pl.multiple_of(i * step, step), step)
        high[at, :], low[at, :] = halves(src[at, :])


def product(ah, al, bh, bl, cols):
    left_h, left_l = ah, al
    rh, rl = bh[:, cols], bl[:, cols]
    return jnp.dot(
        jnp.concatenate([left_h, left_h, left_l], axis=1),
        jnp.concatenate([rh, rl, rh], axis=0),
        preferred_element_type=F32,
    )


def wait(ref, sem):
    pltpu.make_async_copy(ref, ref, sem).wait()


def kernel(
    a_ref, l_ref, r_ref, source, count, windex, wtable,
    iso_ref, env_ref,
    lh, ll, rh, rl, xh, xl, yh, yl, uh, ul, part, x, g, w,
    ga, rs, mine, cb, co, cf,
    z_send, z_recv, s1_send, s1_recv, s2_send, s2_recv, sib_send, sib_recv,
    rs_send, rs_recv, c1_send, c1_recv, c2_send, c2_recv, c3_send, c3_recv,
):
    t = lax.axis_index("terms")
    r = lax.axis_index("rows")
    core = t % 2
    cy = (t // 2) % 4
    zl = (t // 8) % 2
    cx = t // 16
    pos = cx * 4 + cy
    dq = zl * 2 + core
    q = jnp.where(pos % 2 == 1, 3 - dq, dq)
    is_owner = q < 3
    own = jnp.minimum(pos * 3 + q, OWNERS - 1)

    def term(xx, zz, yy, cc):
        return ((xx * 2 + zz) * 4 + yy) * 2 + cc

    def owner_term(m):
        p = m // 3
        qq = m % 3
        d = jnp.where(p % 2 == 1, 3 - qq, qq)
        return term(p // 4, d // 2, p % 4, d % 2)

    def chunk(ref, m, row0=0):
        rows = pl.ds(pl.multiple_of(row0 + (m // 2) * TR, TR), TR)
        return ref.at[rows, pl.ds(pl.multiple_of((m % 2) * TC, TC), TC)]

    def there(tt, rr):
        return {"terms": tt, "rows": rr}

    def remote(src, dst, send, recv, tt, rr):
        return pltpu.make_async_remote_copy(
            src_ref=src, dst_ref=dst, send_sem=send, recv_sem=recv,
            device_id=there(tt, rr), device_id_type=MESH,
        )

    barrier = pltpu.get_barrier_semaphore()

    @pl.loop(1, 64)
    def _(i):
        pl.semaphore_signal(barrier, inc=1, device_id=there((t + i) % 64, r), device_id_type=MESH)

    for dr in range(1, 4):
        for zz in range(2):
            for cc in range(2):
                pl.semaphore_signal(
                    barrier, inc=1, device_id=there(term(cx, zz, cy, cc), (r + dr) % 4), device_id_type=MESH
                )
    pl.semaphore_wait(barrier, 75)

    def to_owners(src, dst, send, recv):
        @pl.loop(0, OWNERS)
        def _(i):
            m = (i + own) % OWNERS
            o = owner_term(m)
            slot = (t - o + 63) % 64

            @pl.when(o != t)
            def _():
                remote(chunk(src, m), dst.at[slot], send, recv, o, r).start()

        @pl.when(is_owner)
        def _():
            dst[63] = chunk(src, own)[...]

    def to_owners_sent(send):
        @pl.when(is_owner)
        def _():
            wait(cb.at[pl.ds(0, 47)], send)

        @pl.when(jnp.logical_not(is_owner))
        def _():
            wait(cb.at[pl.ds(0, 48)], send)

    side_b = jnp.where(core == 0, cx, cy)
    side_a = jnp.where(core == 0, cy, cx)
    here = side_b * 4 + side_a
    right, left, opposite = (side_b + 1) % 4, (side_b + 3) % 4, (side_b + 2) % 4
    kk = 4 * jnp.minimum(q, 2) + r
    to_core = kk // 6
    to_slot = kk % 6
    to_pos = jnp.where(to_core == 0, cx * 4 + cy, cy * 4 + cx)

    def partner(bb, aa):
        return term(jnp.where(core == 0, bb, aa), zl, jnp.where(core == 0, aa, bb), core)

    sibling = term(cx, zl, cy, 1 - core)

    def half(f, cc, bb, hh):
        return ga.at[f, cc, pl.ds(bb * 4 + 2 * hh, 2)]

    def gather_start(f):
        @pl.when(is_owner)
        def _():
            for dz in range(2):
                for dr in range(4):
                    tt, rr = term(cx, (zl + dz) % 2, cy, to_core), (r + dr) % 4
                    dst = ga.at[f, to_core, to_pos, to_slot]
                    if dz == 0 and dr == 0:
                        @pl.when(to_core == core)
                        def _():
                            pltpu.make_async_copy(mine.at[f], dst, z_recv.at[f, to_slot]).start()

                        @pl.when(to_core != core)
                        def _():
                            remote(mine.at[f], dst, z_send.at[f], z_recv.at[f, to_slot], tt, rr).start()
                    else:
                        remote(mine.at[f], dst, z_send.at[f], z_recv.at[f, to_slot], tt, rr).start()

    def gather_rest(f):
        for i in range(6):
            wait(ga.at[f, core, here, i], z_recv.at[f, i])
        block = ga.at[f, core, here]
        for d in range(1, 4):
            remote(block, block, s1_send.at[f], s1_recv.at[f, d - 1], partner(side_b, (side_a + d) % 4), r).start()
        for d in range(1, 4):
            wait(ga.at[f, core, side_b * 4 + (side_a + 4 - d) % 4], s1_recv.at[f, d - 1])

        def push(src, tt, sem):
            remote(src, src, s2_send.at[f], s2_recv.at[f, sem], tt, r).start()

        def across(src, sem):
            remote(src, src, sib_send.at[f], sib_recv.at[f, sem], sibling, r).start()

        to_right, to_left = partner(right, side_a), partner(left, side_a)
        push(half(f, core, side_b, 0), to_right, 0)
        push(half(f, core, side_b, 1), to_left, 2)
        push(half(f, core, side_b, 1), to_right, 1)
        push(half(f, core, side_b, 0), to_left, 3)
        across(ga.at[f, core, pl.ds(side_b * 4, 4)], 0)
        wait(half(f, core, left, 0), s2_recv.at[f, 0])
        push(half(f, core, left, 0), to_right, 4)
        wait(half(f, core, right, 1), s2_recv.at[f, 2])
        push(half(f, core, right, 1), to_left, 5)
        across(half(f, core, left, 0), 1)
        across(half(f, core, right, 1), 2)
        wait(half(f, core, left, 1), s2_recv.at[f, 1])
        across(half(f, core, left, 1), 3)
        wait(half(f, core, right, 0), s2_recv.at[f, 3])
        across(half(f, core, right, 0), 4)
        wait(half(f, core, opposite, 0), s2_recv.at[f, 4])
        across(half(f, core, opposite, 0), 5)
        wait(half(f, core, opposite, 1), s2_recv.at[f, 5])
        across(half(f, core, opposite, 1), 6)
        sb = side_a
        sr, sl, so = (sb + 1) % 4, (sb + 3) % 4, (sb + 2) % 4
        oc = 1 - core
        wait(ga.at[f, oc, pl.ds(sb * 4, 4)], sib_recv.at[f, 0])
        wait(half(f, oc, sl, 0), sib_recv.at[f, 1])
        wait(half(f, oc, sr, 1), sib_recv.at[f, 2])
        wait(half(f, oc, sl, 1), sib_recv.at[f, 3])
        wait(half(f, oc, sr, 0), sib_recv.at[f, 4])
        wait(half(f, oc, so, 0), sib_recv.at[f, 5])
        wait(half(f, oc, so, 1), sib_recv.at[f, 6])

    def gather_sent(f):
        @pl.when(is_owner)
        def _():
            @pl.when(to_core == core)
            def _():
                wait(cb.at[pl.ds(0, 7)], z_send.at[f])

            @pl.when(to_core != core)
            def _():
                wait(cb.at[pl.ds(0, 8)], z_send.at[f])

        wait(ga.at[f, 0, pl.ds(0, 3)], s1_send.at[f])
        wait(ga.at[f, 0, pl.ds(0, 12)], s2_send.at[f])
        wait(ga.at[f, 0], sib_send.at[f])

    def assemble(f):
        for cc in range(2):
            @pl.loop(0, 16)
            def _(s):
                p = s if cc == 0 else (s % 4) * 4 + s // 4
                for i in range(6):
                    k = 6 * cc + i
                    m = p * 3 + k // 4
                    chunk(x, m, (k % 4) * SLAB)[...] = ga[f, cc, s, i]

    def apply_terms():
        split(x, xh, xl, K, 64)

        @pl.loop(0, 3)
        def _(n):
            cols = pl.ds(pl.multiple_of(n * 256, 256), 256)
            uh[:, cols], ul[:, cols] = halves(product(lh[...], ll[...], xh, xl, cols))

        @pl.loop(0, 3)
        def _(n):
            cols = pl.ds(pl.multiple_of(n * 256, 256), 256)
            part[:, cols] = product(uh[...], ul[...], rh, rl, cols)

    @pl.when(is_owner)
    def _():
        mine[0] = chunk(a_ref, own)[...]

    gather_start(0)
    to_owners(l_ref, cb, c1_send, c1_recv)
    split(l_ref, lh, ll, SLAB, 48)
    split(r_ref, rh, rl, K, 64)
    gather_rest(0)

    ring_right, ring_left, ring_far = (r + 1) % 4, (r + 3) % 4, (r + 2) % 4

    def slab_half(rr, hh):
        return cf.at[pl.ds(pl.multiple_of(rr * SLAB + hh * 96, 96), 96)]

    for f in range(2):
        assemble(f)
        apply_terms()
        to_owners(part, rs.at[f], rs_send.at[f], rs_recv.at[f])
        if f == 0:
            @pl.when(is_owner)
            def _():
                wait(cb.at[pl.ds(0, 63)], c1_recv)

                @pl.loop(0, 64)
                def _(i):
                    j = (i + t) % 64
                    total = jnp.zeros((TR, TC), F32)
                    for c in range(FAN):
                        weight = jnp.where(c < count[j], wtable[windex[j, c]], 0.0)
                        total = total + weight * cb[(source[j, c] - t + 63) % 64]
                    co[j] = total
                    dst = chunk(cf, own, r * SLAB)

                    @pl.when(j != t)
                    def _():
                        remote(co.at[j], dst, c2_send, c2_recv, j, r).start()

                    @pl.when(j == t)
                    def _():
                        pltpu.make_async_copy(co.at[j], dst, c2_recv).start()
        else:
            wait(cf.at[pl.ds(pl.multiple_of(r * SLAB, SLAB), SLAB)], c2_recv)
            for hh, rr, sem in ((0, ring_right, 0), (1, ring_left, 2), (1, ring_right, 1), (0, ring_left, 3)):
                remote(slab_half(r, hh), slab_half(r, hh), c3_send, c3_recv.at[sem], t, rr).start()

        @pl.when(is_owner)
        def _():
            wait(rs.at[f, pl.ds(0, 63)], rs_recv.at[f])
            total = lax.fori_loop(0, 64, lambda i, s: s + rs[f, i], jnp.zeros((TR, TC), F32))
            mine[f + 1] = mine[f] - 0.3 * total

        to_owners_sent(rs_send.at[f])
        gather_start(f + 1)
        gather_rest(f + 1)

    assemble(2)
    squares = jnp.sum(lax.fori_loop(
        0, 96, lambda i, s: s + x[pl.ds(pl.multiple_of(i * 8, 8), 8), :] ** 2, jnp.zeros((8, K), F32)
    ))
    scale = 1.0 / jnp.sqrt(jnp.full((8, 128), squares, F32))[0:1, 0:1]

    @pl.loop(0, 12)
    def _(i):
        at = pl.ds(pl.multiple_of(i * 64, 64), 64)
        x[at, :] = x[at, :] * scale

    def transposed(src, high, low):
        @pl.loop(0, 3)
        def _(i):
            for n in range(3):
                at = pl.ds(pl.multiple_of(i * 256, 256), 256)
                to = pl.ds(n * 256, 256)
                high[to, at], low[to, at] = halves(src[at, to].T)

    for sweep in range(SWEEPS):
        split(x, xh, xl, K, 64)
        transposed(x, yh, yl)

        @pl.loop(0, 3)
        def _(n):
            cols = pl.ds(pl.multiple_of(n * 256, 256), 256)
            g[:, cols] = product(yh[...], yl[...], xh, xl, cols)

        split(g, yh, yl, K, 64)

        @pl.loop(0, 3)
        def _(n):
            cols = pl.ds(pl.multiple_of(n * 256, 256), 256)
            w[:, cols] = COEF_TWO * g[:, cols] + COEF_THREE * product(yh[...], yl[...], yh, yl, cols)

        split(w, yh, yl, K, 64)

        @pl.loop(0, 3)
        def _(n):
            cols = pl.ds(pl.multiple_of(n * 256, 256), 256)
            x[:, cols] = COEF_ONE * x[:, cols] + product(xh[...], xl[...], yh, yl, cols)

        if sweep == 0:
            wait(slab_half(ring_left, 0), c3_recv.at[0])
            remote(slab_half(ring_left, 0), slab_half(ring_left, 0), c3_send, c3_recv.at[4], t, ring_right).start()
            wait(slab_half(ring_right, 1), c3_recv.at[2])
            remote(slab_half(ring_right, 1), slab_half(ring_right, 1), c3_send, c3_recv.at[5], t, ring_left).start()

    @pl.loop(0, 12)
    def _(i):
        at = pl.ds(pl.multiple_of(i * 64, 64), 64)
        x[at, :] = x[at, :] * math.sqrt(K)

    my_rows = pl.ds(pl.multiple_of(r * SLAB, SLAB), SLAB)
    iso_ref[...] = x[my_rows, :]
    transposed(x, yh, yl)
    lh[...] = yh[my_rows, :]
    ll[...] = yl[my_rows, :]
    split(x, xh, xl, K, 64)
    for rr, hh, sem in ((ring_left, 1, 1), (ring_right, 0, 3), (ring_far, 0, 4), (ring_far, 1, 5)):
        wait(slab_half(rr, hh), c3_recv.at[sem])
    split(cf, rh, rl, K, 64)

    @pl.loop(0, 3)
    def _(n):
        cols = pl.ds(pl.multiple_of(n * 256, 256), 256)
        uh[:, cols], ul[:, cols] = halves(product(lh[...], ll[...], rh, rl, cols))

    @pl.loop(0, 3)
    def _(n):
        cols = pl.ds(pl.multiple_of(n * 256, 256), 256)
        env_ref[:, cols] = product(uh[...], ul[...], xh, xl, cols)

    for f in range(3):
        gather_sent(f)
    to_owners_sent(c1_send)

    @pl.when(is_owner)
    def _():
        wait(co.at[pl.ds(0, 63)], c2_send)

    wait(cf.at[pl.ds(0, 3 * SLAB)], c3_send)


def body(amplitudes, left_terms, right_terms, source_list, list_count, weight_index, weight_table):
    vmem = pl.BlockSpec(memory_space=pltpu.VMEM)
    smem = pl.BlockSpec(memory_space=pltpu.SMEM)
    dma = pltpu.SemaphoreType.DMA
    slab = jax.ShapeDtypeStruct((SLAB, K), F32)
    iso, env = pl.pallas_call(
        kernel,
        out_shape=(slab, slab),
        in_specs=[vmem] * 3 + [smem] * 4,
        out_specs=(vmem, vmem),
        scratch_shapes=[
            pltpu.VMEM((SLAB, K), BF), pltpu.VMEM((SLAB, K), BF),
            pltpu.VMEM((K, K), BF), pltpu.VMEM((K, K), BF),
            pltpu.VMEM((K, K), BF), pltpu.VMEM((K, K), BF),
            pltpu.VMEM((K, K), BF), pltpu.VMEM((K, K), BF),
            pltpu.VMEM((SLAB, K), BF), pltpu.VMEM((SLAB, K), BF),
            pltpu.VMEM((SLAB, K), F32),
            pltpu.VMEM((K, K), F32), pltpu.VMEM((K, K), F32), pltpu.VMEM((K, K), F32),
            pltpu.VMEM((3, 2, 16, 6, TR, TC), F32),
            pltpu.VMEM((2, 64, TR, TC), F32),
            pltpu.VMEM((3, TR, TC), F32),
            pltpu.VMEM((64, TR, TC), F32),
            pltpu.VMEM((64, TR, TC), F32),
            pltpu.VMEM((K, K), F32),
            dma((3,)), dma((3, 6)), dma((3,)), dma((3, 3)), dma((3,)), dma((3, 6)), dma((3,)), dma((3, 7)),
            dma((2,)), dma((2,)), dma, dma, dma, dma, dma, dma((6,)),
        ],
        compiler_params=pltpu.CompilerParams(
            collective_id=0, has_side_effects=True, vmem_limit_bytes=56 * 1024 * 1024
        ),
        cost_estimate=pl.CostEstimate(flops=28 * 10**9, bytes_accessed=8 * 10**6, transcendentals=0),
    )(
        amplitudes, left_terms.reshape(SLAB, K), right_terms.reshape(K, K),
        source_list, list_count, weight_index, weight_table,
    )
    return iso, env.reshape(1, SLAB, K)


def solution(mesh):
    placed = (P("rows", None), P("terms", "rows", None), P("terms", None, None), P(), P(), P(), P())
    return jax.shard_map(
        body,
        mesh=mesh,
        in_specs=placed,
        out_specs=(P("rows", None), P("terms", "rows", None)),
        check_vma=False,
    )
```

```python
import math

import jax
import jax.numpy as jnp
from jax import lax
from jax.experimental import pallas as pl
from jax.experimental.pallas import tpu as pltpu
from jax.sharding import PartitionSpec as P

K = 768
FAN = 4
SWEEPS = 3
SLAB = 192
OWNERS = 48
TR, TC = 8, 384
COEF_ONE = 3.4445
COEF_TWO = -4.775
COEF_THREE = 2.0315
MESH = pl.DeviceIdType.MESH
BF = jnp.bfloat16
F32 = jnp.float32


def halves(value):
    high = value.astype(BF)
    return high, (value - high.astype(F32)).astype(BF)


def split(src, high, low, rows, step):
    @pl.loop(0, rows // step)
    def _(i):
        at = pl.ds(pl.multiple_of(i * step, step), step)
        high[at, :], low[at, :] = halves(src[at, :])


def product(ah, al, bh, bl, cols):
    left_h, left_l = ah, al
    rh, rl = bh[:, cols], bl[:, cols]
    return jnp.dot(
        jnp.concatenate([left_h, left_h, left_l], axis=1),
        jnp.concatenate([rh, rl, rh], axis=0),
        preferred_element_type=F32,
    )


def wait(ref, sem):
    pltpu.make_async_copy(ref, ref, sem).wait()


def kernel(
    a_ref, l_hbm, r_hbm, source, count, windex, wtable,
    iso_ref, env_ref,
    lh, ll, rh, rl, xh, xl, yh, yl, uh, ul, part, x, g, w,
    ga, rs, mine, cb, co, cf, l_ref, in_sem,
    z_send, z_recv, s1_send, s1_recv, s2_send, s2_recv, sib_send, sib_recv,
    rs_send, rs_recv, c1_send, c1_recv, c2_send, c2_recv, c3_send, c3_recv,
):
    t = lax.axis_index("terms")
    r = lax.axis_index("rows")
    core = t % 2
    cy = (t // 2) % 4
    zl = (t // 8) % 2
    cx = t // 16
    pos = cx * 4 + cy
    dq = zl * 2 + core
    q = jnp.where(pos % 2 == 1, 3 - dq, dq)
    is_owner = q < 3
    own = jnp.minimum(pos * 3 + q, OWNERS - 1)

    def term(xx, zz, yy, cc):
        return ((xx * 2 + zz) * 4 + yy) * 2 + cc

    def owner_term(m):
        p = m // 3
        qq = m % 3
        d = jnp.where(p % 2 == 1, 3 - qq, qq)
        return term(p // 4, d // 2, p % 4, d % 2)

    def chunk(ref, m, row0=0):
        rows = pl.ds(pl.multiple_of(row0 + (m // 2) * TR, TR), TR)
        return ref.at[rows, pl.ds(pl.multiple_of((m % 2) * TC, TC), TC)]

    def there(tt, rr):
        return {"terms": tt, "rows": rr}

    def remote(src, dst, send, recv, tt, rr):
        return pltpu.make_async_remote_copy(
            src_ref=src, dst_ref=dst, send_sem=send, recv_sem=recv,
            device_id=there(tt, rr), device_id_type=MESH,
        )

    bring_l = pltpu.make_async_copy(l_hbm, l_ref, in_sem.at[0])
    bring_r = pltpu.make_async_copy(r_hbm, w, in_sem.at[1])
    bring_l.start()
    bring_r.start()
    barrier = pltpu.get_barrier_semaphore()

    @pl.loop(1, 64)
    def _(i):
        pl.semaphore_signal(barrier, inc=1, device_id=there((t + i) % 64, r), device_id_type=MESH)

    for dr in range(1, 4):
        for zz in range(2):
            for cc in range(2):
                pl.semaphore_signal(
                    barrier, inc=1, device_id=there(term(cx, zz, cy, cc), (r + dr) % 4), device_id_type=MESH
                )
    bring_l.wait()
    split(l_ref, lh, ll, SLAB, 48)
    bring_r.wait()
    split(w, rh, rl, K, 64)
    pl.semaphore_wait(barrier, 75)

    def to_owners(src, dst, send, recv, side):
        @pl.loop(0, OWNERS // 2)
        def _(i):
            m = 2 * ((i + own // 2) % (OWNERS // 2)) + side
            o = owner_term(m)
            slot = (t - o + 63) % 64

            @pl.when(o != t)
            def _():
                remote(chunk(src, m), dst.at[slot], send, recv, o, r).start()

        if side == 1:
            @pl.when(is_owner)
            def _():
                dst[63] = chunk(src, own)[...]

    def to_owners_sent(send):
        @pl.when(is_owner)
        def _():
            wait(cb.at[pl.ds(0, 47)], send)

        @pl.when(jnp.logical_not(is_owner))
        def _():
            wait(cb.at[pl.ds(0, 48)], send)

    side_b = jnp.where(core == 0, cx, cy)
    side_a = jnp.where(core == 0, cy, cx)
    here = side_b * 4 + side_a
    right, left, opposite = (side_b + 1) % 4, (side_b + 3) % 4, (side_b + 2) % 4
    kk = 4 * jnp.minimum(q, 2) + r
    to_core = kk // 6
    to_slot = kk % 6
    to_pos = jnp.where(to_core == 0, cx * 4 + cy, cy * 4 + cx)

    def partner(bb, aa):
        return term(jnp.where(core == 0, bb, aa), zl, jnp.where(core == 0, aa, bb), core)

    sibling = term(cx, zl, cy, 1 - core)

    def gather_start(f):
        @pl.when(is_owner)
        def _():
            for dz in range(2):
                for dr in range(4):
                    tt, rr = term(cx, (zl + dz) % 2, cy, to_core), (r + dr) % 4
                    dst = ga.at[f, to_core, to_pos, to_slot]
                    if dz == 0 and dr == 0:
                        @pl.when(to_core == core)
                        def _():
                            pltpu.make_async_copy(mine.at[f], dst, z_recv.at[f, to_slot]).start()

                        @pl.when(to_core != core)
                        def _():
                            remote(mine.at[f], dst, z_send.at[f], z_recv.at[f, to_slot], tt, rr).start()
                    else:
                        remote(mine.at[f], dst, z_send.at[f], z_recv.at[f, to_slot], tt, rr).start()

    def gather_rest(f):
        for i in range(6):
            wait(ga.at[f, core, here, i], z_recv.at[f, i])

        def block(bb, d):
            return ga.at[f, core, bb * 4 + (side_a + 4 - d) % 4]

        def across(bb, d, sem):
            remote(block(bb, d), block(bb, d), sib_send.at[f], sib_recv.at[f, sem], sibling, r).start()

        def push(bb, d, tt, sem):
            remote(block(bb, d), block(bb, d), s2_send.at[f], s2_recv.at[f, sem], tt, r).start()

        to_right, to_left = partner(right, side_a), partner(left, side_a)
        mine_now = block(side_b, 0)
        for d in (1, 3, 2):
            remote(mine_now, mine_now, s1_send.at[f], s1_recv.at[f, d - 1], partner(side_b, (side_a + d) % 4), r).start()
        order = (0, 1, 3, 2)
        for d in order:
            if d > 0:
                wait(block(side_b, d), s1_recv.at[f, d - 1])
            push(side_b, d, to_right, d)
            push(side_b, d, to_left, 4 + d)
            across(side_b, d, d)
        for d in order:
            wait(block(left, d), s2_recv.at[f, d])
            if d in (0, 3):
                push(left, d, to_right, 8 + d)
            wait(block(right, d), s2_recv.at[f, 4 + d])
            if d in (1, 2):
                push(right, d, to_left, 8 + d)
            across(left, d, 4 + d)
            across(right, d, 8 + d)
        for d in order:
            wait(block(opposite, d), s2_recv.at[f, 8 + d])
            across(opposite, d, 12 + d)
        for n, bb in enumerate((side_a, (side_a + 3) % 4, (side_a + 1) % 4, (side_a + 2) % 4)):
            for d in order:
                wait(ga.at[f, 1 - core, bb * 4 + (side_b + 4 - d) % 4], sib_recv.at[f, 4 * n + d])

    def gather_sent(f):
        @pl.when(is_owner)
        def _():
            @pl.when(to_core == core)
            def _():
                wait(cb.at[pl.ds(0, 7)], z_send.at[f])

            @pl.when(to_core != core)
            def _():
                wait(cb.at[pl.ds(0, 8)], z_send.at[f])

        wait(ga.at[f, 0, pl.ds(0, 3)], s1_send.at[f])
        wait(ga.at[f, 0, pl.ds(0, 12)], s2_send.at[f])
        wait(ga.at[f, 0], sib_send.at[f])

    def assemble(f):
        for cc in range(2):
            @pl.loop(0, 16)
            def _(s):
                p = s if cc == 0 else (s % 4) * 4 + s // 4
                for i in range(6):
                    k = 6 * cc + i
                    m = p * 3 + k // 4
                    chunk(x, m, (k % 4) * SLAB)[...] = ga[f, cc, s, i]

    def apply_terms(f):
        split(x, xh, xl, K, 64)

        @pl.loop(0, 3)
        def _(n):
            cols = pl.ds(pl.multiple_of(n * 256, 256), 256)
            uh[:, cols], ul[:, cols] = halves(product(lh[...], ll[...], xh, xl, cols))

        for side, tiles in ((0, 2), (1, 1)):
            @pl.loop(0, tiles)
            def _(n):
                cols = pl.ds(pl.multiple_of((n + 2 * side) * 256, 256), 256)
                part[:, cols] = product(uh[...], ul[...], rh, rl, cols)

            to_owners(part, rs.at[f], rs_send.at[f], rs_recv.at[f], side)

    @pl.when(is_owner)
    def _():
        mine[0] = chunk(a_ref, own)[...]

    gather_start(0)
    to_owners(l_ref, cb, c1_send, c1_recv, 0)
    to_owners(l_ref, cb, c1_send, c1_recv, 1)
    gather_rest(0)

    ring_right, ring_left, ring_far = (r + 1) % 4, (r + 3) % 4, (r + 2) % 4

    def slab_half(rr, hh):
        return cf.at[pl.ds(pl.multiple_of(rr * SLAB + hh * 96, 96), 96)]

    for f in range(2):
        assemble(f)
        apply_terms(f)
        if f == 0:
            @pl.when(is_owner)
            def _():
                wait(cb.at[pl.ds(0, 63)], c1_recv)

                @pl.loop(0, 64)
                def _(i):
                    j = (i + t) % 64
                    total = jnp.zeros((TR, TC), F32)
                    for c in range(FAN):
                        weight = jnp.where(c < count[j], wtable[windex[c, j]], 0.0)
                        total = total + weight * cb[(source[c, j] - t + 63) % 64]
                    co[j] = total
                    dst = chunk(cf, own, r * SLAB)

                    @pl.when(j != t)
                    def _():
                        remote(co.at[j], dst, c2_send, c2_recv, j, r).start()

                    @pl.when(j == t)
                    def _():
                        pltpu.make_async_copy(co.at[j], dst, c2_recv).start()
        else:
            wait(slab_half(ring_left, 0), c3_recv.at[0])
            remote(slab_half(ring_left, 0), slab_half(ring_left, 0), c3_send, c3_recv.at[4], t, ring_right).start()
            wait(slab_half(ring_right, 1), c3_recv.at[2])
            remote(slab_half(ring_right, 1), slab_half(ring_right, 1), c3_send, c3_recv.at[5], t, ring_left).start()

        @pl.when(is_owner)
        def _():
            wait(rs.at[f, pl.ds(0, 63)], rs_recv.at[f])
            total = lax.fori_loop(0, 64, lambda i, s: s + rs[f, i], jnp.zeros((TR, TC), F32))
            mine[f + 1] = mine[f] - 0.3 * total

        to_owners_sent(rs_send.at[f])
        gather_start(f + 1)
        if f == 0:
            wait(cf.at[pl.ds(pl.multiple_of(r * SLAB, SLAB), SLAB)], c2_recv)
            for hh, rr, sem in ((0, ring_right, 0), (1, ring_left, 2), (1, ring_right, 1), (0, ring_left, 3)):
                remote(slab_half(r, hh), slab_half(r, hh), c3_send, c3_recv.at[sem], t, rr).start()
        gather_rest(f + 1)

    assemble(2)
    squares = jnp.sum(lax.fori_loop(
        0, 96, lambda i, s: s + x[pl.ds(pl.multiple_of(i * 8, 8), 8), :] ** 2, jnp.zeros((8, K), F32)
    ))
    scale = 1.0 / jnp.sqrt(jnp.full((8, 128), squares, F32))[0:1, 0:1]

    @pl.loop(0, 12)
    def _(i):
        at = pl.ds(pl.multiple_of(i * 64, 64), 64)
        x[at, :] = x[at, :] * scale

    def transposed(src, high, low):
        @pl.loop(0, 3)
        def _(i):
            for n in range(3):
                at = pl.ds(pl.multiple_of(i * 256, 256), 256)
                to = pl.ds(n * 256, 256)
                high[to, at], low[to, at] = halves(src[at, to].T)

    for sweep in range(SWEEPS):
        split(x, xh, xl, K, 64)
        transposed(x, yh, yl)

        @pl.loop(0, 3)
        def _(n):
            cols = pl.ds(pl.multiple_of(n * 256, 256), 256)
            g[:, cols] = product(yh[...], yl[...], xh, xl, cols)

        split(g, yh, yl, K, 64)

        @pl.loop(0, 3)
        def _(n):
            cols = pl.ds(pl.multiple_of(n * 256, 256), 256)
            w[:, cols] = COEF_TWO * g[:, cols] + COEF_THREE * product(yh[...], yl[...], yh, yl, cols)

        split(w, yh, yl, K, 64)

        @pl.loop(0, 3)
        def _(n):
            cols = pl.ds(pl.multiple_of(n * 256, 256), 256)
            x[:, cols] = COEF_ONE * x[:, cols] + product(xh[...], xl[...], yh, yl, cols)

    @pl.loop(0, 12)
    def _(i):
        at = pl.ds(pl.multiple_of(i * 64, 64), 64)
        x[at, :] = x[at, :] * math.sqrt(K)

    my_rows = pl.ds(pl.multiple_of(r * SLAB, SLAB), SLAB)
    iso_ref[...] = x[my_rows, :]
    transposed(x, yh, yl)
    lh[...] = yh[my_rows, :]
    ll[...] = yl[my_rows, :]
    split(x, xh, xl, K, 64)
    for rr, hh, sem in ((ring_left, 1, 1), (ring_right, 0, 3), (ring_far, 0, 4), (ring_far, 1, 5)):
        wait(slab_half(rr, hh), c3_recv.at[sem])
    split(cf, rh, rl, K, 64)

    @pl.loop(0, 3)
    def _(n):
        cols = pl.ds(pl.multiple_of(n * 256, 256), 256)
        uh[:, cols], ul[:, cols] = halves(product(lh[...], ll[...], rh, rl, cols))

    @pl.loop(0, 3)
    def _(n):
        cols = pl.ds(pl.multiple_of(n * 256, 256), 256)
        env_ref[:, cols] = product(uh[...], ul[...], xh, xl, cols)

    for f in range(3):
        gather_sent(f)
    to_owners_sent(c1_send)

    @pl.when(is_owner)
    def _():
        wait(co.at[pl.ds(0, 63)], c2_send)

    wait(cf.at[pl.ds(0, 3 * SLAB)], c3_send)


def body(amplitudes, left_terms, right_terms, source_list, list_count, weight_index, weight_table):
    vmem = pl.BlockSpec(memory_space=pltpu.VMEM)
    smem = pl.BlockSpec(memory_space=pltpu.SMEM)
    dma = pltpu.SemaphoreType.DMA
    slab = jax.ShapeDtypeStruct((SLAB, K), F32)
    iso, env = pl.pallas_call(
        kernel,
        out_shape=(slab, slab),
        in_specs=[vmem] + [pl.BlockSpec(memory_space=pl.ANY)] * 2 + [smem] * 4,
        out_specs=(vmem, vmem),
        scratch_shapes=[
            pltpu.VMEM((SLAB, K), BF), pltpu.VMEM((SLAB, K), BF),
            pltpu.VMEM((K, K), BF), pltpu.VMEM((K, K), BF),
            pltpu.VMEM((K, K), BF), pltpu.VMEM((K, K), BF),
            pltpu.VMEM((K, K), BF), pltpu.VMEM((K, K), BF),
            pltpu.VMEM((SLAB, K), BF), pltpu.VMEM((SLAB, K), BF),
            pltpu.VMEM((SLAB, K), F32),
            pltpu.VMEM((K, K), F32), pltpu.VMEM((K, K), F32), pltpu.VMEM((K, K), F32),
            pltpu.VMEM((3, 2, 16, 6, TR, TC), F32),
            pltpu.VMEM((2, 64, TR, TC), F32),
            pltpu.VMEM((3, TR, TC), F32),
            pltpu.VMEM((64, TR, TC), F32),
            pltpu.VMEM((64, TR, TC), F32),
            pltpu.VMEM((K, K), F32),
            pltpu.VMEM((SLAB, K), F32),
            dma((2,)),
            dma((3,)), dma((3, 6)), dma((3,)), dma((3, 3)), dma((3,)), dma((3, 12)), dma((3,)), dma((3, 16)),
            dma((2,)), dma((2,)), dma, dma, dma, dma, dma, dma((6,)),
        ],
        compiler_params=pltpu.CompilerParams(
            collective_id=0, has_side_effects=True, vmem_limit_bytes=56 * 1024 * 1024
        ),
        cost_estimate=pl.CostEstimate(flops=28 * 10**9, bytes_accessed=8 * 10**6, transcendentals=0),
    )(
        amplitudes, left_terms.reshape(SLAB, K), right_terms.reshape(K, K),
        source_list.T, list_count, weight_index.T, weight_table,
    )
    return iso, env.reshape(1, SLAB, K)


def solution(mesh):
    placed = (P("rows", None), P("terms", "rows", None), P("terms", None, None), P(), P(), P(), P())
    return jax.shard_map(
        body,
        mesh=mesh,
        in_specs=placed,
        out_specs=(P("rows", None), P("terms", "rows", None)),
        check_vma=False,
    )
```

```python
import math

import jax
import jax.numpy as jnp
from jax import lax
from jax.experimental import pallas as pl
from jax.experimental.pallas import tpu as pltpu
from jax.sharding import PartitionSpec as P

K = 768
FAN = 4
SWEEPS = 3
SLAB = 192
OWNERS = 48
TR, TC = 8, 384
COEF_ONE = 3.4445
COEF_TWO = -4.775
COEF_THREE = 2.0315
MESH = pl.DeviceIdType.MESH
BF = jnp.bfloat16
F32 = jnp.float32


def halves(value):
    high = value.astype(BF)
    return high, (value - high.astype(F32)).astype(BF)


def split(src, high, low, rows, step):
    @pl.loop(0, rows // step)
    def _(i):
        at = pl.ds(pl.multiple_of(i * step, step), step)
        high[at, :], low[at, :] = halves(src[at, :])


def product(ah, al, bh, bl, cols):
    left_h, left_l = ah, al
    rh, rl = bh[:, cols], bl[:, cols]
    return jnp.dot(
        jnp.concatenate([left_h, left_h, left_l], axis=1),
        jnp.concatenate([rh, rl, rh], axis=0),
        preferred_element_type=F32,
    )


def wait(ref, sem):
    pltpu.make_async_copy(ref, ref, sem).wait()


def kernel(
    a_ref, l_hbm, r_hbm, source, count, windex, wtable,
    iso_ref, env_ref,
    lh, ll, rh, rl, xh, xl, vh, vl, yh, yl, gh, gl, wh, wl, uh, ul, part, x, w, pre,
    ga, rs, mine, cb, co, cf, l_ref, in_sem,
    z_send, z_recv, s1_send, s1_recv, s2_send, s2_recv, sib_send, sib_recv,
    pre_send, pre_recv, rs_send, rs_recv, c1_send, c1_recv, c2_send, c2_recv, c3_send, c3_recv,
):
    t = lax.axis_index("terms")
    r = lax.axis_index("rows")
    core = t % 2
    cy = (t // 2) % 4
    zl = (t // 8) % 2
    cx = t // 16
    pos = cx * 4 + cy
    dq = zl * 2 + core
    q = jnp.where(pos % 2 == 1, 3 - dq, dq)
    is_owner = q < 3
    own = jnp.minimum(pos * 3 + q, OWNERS - 1)

    def term(xx, zz, yy, cc):
        return ((xx * 2 + zz) * 4 + yy) * 2 + cc

    def owner_term(m):
        p = m // 3
        qq = m % 3
        d = jnp.where(p % 2 == 1, 3 - qq, qq)
        return term(p // 4, d // 2, p % 4, d % 2)

    def chunk(ref, m, row0=0):
        rows = pl.ds(pl.multiple_of(row0 + (m // 2) * TR, TR), TR)
        return ref.at[rows, pl.ds(pl.multiple_of((m % 2) * TC, TC), TC)]

    def there(tt, rr):
        return {"terms": tt, "rows": rr}

    def remote(src, dst, send, recv, tt, rr):
        return pltpu.make_async_remote_copy(
            src_ref=src, dst_ref=dst, send_sem=send, recv_sem=recv,
            device_id=there(tt, rr), device_id_type=MESH,
        )

    bring_l = pltpu.make_async_copy(l_hbm, l_ref, in_sem.at[0])
    bring_r = pltpu.make_async_copy(r_hbm, w, in_sem.at[1])
    bring_l.start()
    bring_r.start()
    barrier = pltpu.get_barrier_semaphore()

    @pl.loop(1, 64)
    def _(i):
        pl.semaphore_signal(barrier, inc=1, device_id=there((t + i) % 64, r), device_id_type=MESH)

    for dr in range(1, 4):
        for zz in range(2):
            for cc in range(2):
                pl.semaphore_signal(
                    barrier, inc=1, device_id=there(term(cx, zz, cy, cc), (r + dr) % 4), device_id_type=MESH
                )
    bring_l.wait()
    split(l_ref, lh, ll, SLAB, 48)
    bring_r.wait()
    split(w, rh, rl, K, 64)
    pl.semaphore_wait(barrier, 75)

    def to_owners(src, dst, send, recv):
        @pl.loop(0, OWNERS)
        def _(i):
            m = (i + own) % OWNERS
            o = owner_term(m)
            slot = (t - o + 63) % 64

            @pl.when(o != t)
            def _():
                remote(chunk(src, m), dst.at[slot], send, recv, o, r).start()

        @pl.when(is_owner)
        def _():
            dst[63] = chunk(src, own)[...]

    def to_owners_sent(send):
        @pl.when(is_owner)
        def _():
            wait(cb.at[pl.ds(0, 47)], send)

        @pl.when(jnp.logical_not(is_owner))
        def _():
            wait(cb.at[pl.ds(0, 48)], send)

    sibling = term(cx, zl, cy, 1 - core)
    kept = pl.ds(pl.multiple_of(core * 96, 96), 96)
    given = pl.ds(pl.multiple_of((1 - core) * 96, 96), 96)
    keeps_own = jnp.logical_and(is_owner, own // 24 == core)

    def tile(n):
        return pl.ds(n * 256, 256)

    def pre_start(f, n):
        remote(part.at[given, tile(n)], pre.at[f, :, tile(n)], pre_send.at[f], pre_recv.at[f, n], sibling, r).start()

    def pre_add(f, n):
        wait(pre.at[f, :, tile(n)], pre_recv.at[f, n])
        part[kept, tile(n)] = part[kept, tile(n)] + pre[f, :, tile(n)]

    def reduce_start(f, side):
        @pl.loop(0, 12)
        def _(i):
            m = 24 * core + 2 * ((i + pos) % 12) + side
            o = owner_term(m)
            dst = rs.at[f, (t // 2 - o // 2 + 31) % 32]

            @pl.when(o != t)
            def _():
                remote(chunk(part, m), dst, rs_send.at[f], rs_recv.at[f], o, r).start()

            @pl.when(o == t)
            def _():
                pltpu.make_async_copy(chunk(part, m), dst, rs_recv.at[f]).start()

    def reduce_sent(f):
        wait(pre.at[f], pre_send.at[f])

        @pl.when(keeps_own)
        def _():
            wait(rs.at[f, pl.ds(0, 23)], rs_send.at[f])

        @pl.when(jnp.logical_not(keeps_own))
        def _():
            wait(rs.at[f, pl.ds(0, 24)], rs_send.at[f])

    side_b = jnp.where(core == 0, cx, cy)
    side_a = jnp.where(core == 0, cy, cx)
    here = side_b * 4 + side_a
    kk = 4 * jnp.minimum(q, 2) + r
    to_core = kk // 6
    to_slot = kk % 6
    to_pos = jnp.where(to_core == 0, cx * 4 + cy, cy * 4 + cx)

    def partner(bb, aa):
        return term(jnp.where(core == 0, bb, aa), zl, jnp.where(core == 0, aa, bb), core)

    def gather_start(f):
        @pl.when(is_owner)
        def _():
            for dz in range(2):
                for dr in range(4):
                    tt, rr = term(cx, (zl + dz) % 2, cy, to_core), (r + dr) % 4
                    dst = ga.at[f, to_core, to_pos, to_slot]
                    if dz == 0 and dr == 0:
                        @pl.when(to_core == core)
                        def _():
                            pltpu.make_async_copy(mine.at[f], dst, z_recv.at[f, to_slot]).start()

                        @pl.when(to_core != core)
                        def _():
                            remote(mine.at[f], dst, z_send.at[f], z_recv.at[f, to_slot], tt, rr).start()
                    else:
                        remote(mine.at[f], dst, z_send.at[f], z_recv.at[f, to_slot], tt, rr).start()

    def gather_rest(f, after_z=None, after_push=None):
        for i in range(6):
            wait(ga.at[f, core, here, i], z_recv.at[f, i])

        def block(bb, d):
            return ga.at[f, core, bb * 4 + (side_a + 4 - d) % 4]

        def across(bb, d, sem):
            remote(block(bb, d), block(bb, d), sib_send.at[f], sib_recv.at[f, sem], sibling, r).start()

        def push(bb, d, tt, sem):
            remote(block(bb, d), block(bb, d), s2_send.at[f], s2_recv.at[f, sem], tt, r).start()

        mine_now = block(side_b, 0)
        for d in (1, 3, 2):
            remote(mine_now, mine_now, s1_send.at[f], s1_recv.at[f, d - 1], partner(side_b, (side_a + d) % 4), r).start()
        if after_z:
            after_z()
        order = (0, 1, 3, 2)
        for d in order:
            if d > 0:
                wait(block(side_b, d), s1_recv.at[f, d - 1])
            for n in (1, 3, 2):
                push(side_b, d, partner((side_b + n) % 4, side_a), 4 * (n - 1) + d)
            across(side_b, d, d)
        if after_push:
            after_push()
        for n in (1, 3, 2):
            for d in order:
                bb = (side_b + 4 - n) % 4
                wait(block(bb, d), s2_recv.at[f, 4 * (n - 1) + d])
                across(bb, d, 4 * n + d)
        for n in (0, 1, 3, 2):
            for d in order:
                bb = (side_a + 4 - n) % 4
                wait(ga.at[f, 1 - core, bb * 4 + (side_b + 4 - d) % 4], sib_recv.at[f, 4 * n + d])

    def gather_sent(f):
        @pl.when(is_owner)
        def _():
            @pl.when(to_core == core)
            def _():
                wait(cb.at[pl.ds(0, 7)], z_send.at[f])

            @pl.when(to_core != core)
            def _():
                wait(cb.at[pl.ds(0, 8)], z_send.at[f])

        wait(ga.at[f, 0, pl.ds(0, 3)], s1_send.at[f])
        wait(ga.at[f, 0, pl.ds(0, 12)], s2_send.at[f])
        wait(ga.at[f, 0], sib_send.at[f])

    def assemble(f):
        for cc in range(2):
            @pl.loop(0, 16)
            def _(s):
                p = s if cc == 0 else (s % 4) * 4 + s // 4
                for i in range(6):
                    k = 6 * cc + i
                    m = p * 3 + k // 4
                    chunk(x, m, (k % 4) * SLAB)[...] = ga[f, cc, s, i]

    def apply_terms(f):
        split(x, xh, xl, K, 64)

        @pl.loop(0, 3)
        def _(n):
            cols = pl.ds(pl.multiple_of(n * 256, 256), 256)
            uh[:, cols], ul[:, cols] = halves(product(lh[...], ll[...], xh, xl, cols))

        for n in range(3):
            part[:, tile(n)] = product(uh[...], ul[...], rh, rl, tile(n))
            pre_start(f, n)
        pre_add(f, 0)
        pre_add(f, 1)
        reduce_start(f, 0)
        pre_add(f, 2)
        reduce_start(f, 1)

    @pl.when(is_owner)
    def _():
        mine[0] = chunk(a_ref, own)[...]

    gather_start(0)
    to_owners(l_ref, cb, c1_send, c1_recv)
    gather_rest(0)

    ring_right, ring_left, ring_far = (r + 1) % 4, (r + 3) % 4, (r + 2) % 4

    def slab_half(rr, hh):
        return cf.at[pl.ds(pl.multiple_of(rr * SLAB + hh * 96, 96), 96)]

    def go_round(rr, hh, to, sem):
        remote(slab_half(rr, hh), slab_half(rr, hh), c3_send, c3_recv.at[sem], t, to).start()

    def mix():
        @pl.when(is_owner)
        def _():
            wait(cb.at[pl.ds(0, 63)], c1_recv)

            @pl.loop(0, 64)
            def _(j):
                total = jnp.zeros((TR, TC), F32)
                for c in range(FAN):
                    weight = jnp.where(c < count[j], wtable[windex[c, j]], 0.0)
                    total = total + weight * cb[(source[c, j] - t + 63) % 64]
                co[j] = total

    def give_back():
        @pl.when(is_owner)
        def _():
            dst = chunk(cf, own, r * SLAB)

            @pl.loop(1, 64)
            def _(i):
                j = (i + t) % 64
                remote(co.at[j], dst, c2_send, c2_recv, j, r).start()

            pltpu.make_async_copy(co.at[t], dst, c2_recv).start()

    def first_round():
        wait(cf.at[pl.ds(pl.multiple_of(r * SLAB, SLAB), SLAB)], c2_recv)
        go_round(r, 0, ring_right, 0)
        go_round(r, 1, ring_left, 2)

    def second_round():
        go_round(r, 1, ring_right, 1)
        go_round(r, 0, ring_left, 3)
        wait(slab_half(ring_left, 0), c3_recv.at[0])
        go_round(ring_left, 0, ring_right, 4)
        wait(slab_half(ring_right, 1), c3_recv.at[2])
        go_round(ring_right, 1, ring_left, 5)

    for f in range(2):
        assemble(f)
        apply_terms(f)
        if f == 0:
            mix()

        @pl.when(is_owner)
        def _():
            wait(rs.at[f], rs_recv.at[f])
            mine[f + 1] = mine[f] - 0.3 * jnp.sum(rs[f], axis=0)

        gather_start(f + 1)
        if f == 0:
            give_back()
        reduce_sent(f)
        if f == 0:
            gather_rest(1, after_push=first_round)
        else:
            gather_rest(2, after_z=second_round)

    assemble(2)
    squares = jnp.sum(lax.fori_loop(
        0, 12,
        lambda i, s: s + jnp.sum((x[pl.ds(pl.multiple_of(i * 64, 64), 64), :] ** 2).reshape(8, 8, K), axis=0),
        jnp.zeros((8, K), F32),
    ))
    scale = 1.0 / jnp.sqrt(jnp.full((8, 128), squares, F32))[0:1, 0:1]
    for n in range(3):
        value = x[tile(n), :] * scale
        xh[tile(n), :], xl[tile(n), :] = halves(value)
        yh[:, tile(n)], yl[:, tile(n)] = halves(value.T)

    def symmetric(ah, al, bh, bl, oh, ol, last):
        for n in range(3):
            top = 256 * (n + 1)
            value = last(product(ah[:top, :], al[:top, :], bh, bl, tile(n)), n)
            oh[:top, tile(n)], ol[:top, tile(n)] = halves(value)
            for m in range(n):
                oh[tile(n), tile(m)], ol[tile(n), tile(m)] = halves(value[256 * m:256 * (m + 1)].T)

    def polynomial(value, n):
        top = value.shape[0]
        gram = gh[:top, tile(n)].astype(F32) + gl[:top, tile(n)].astype(F32)
        row = lax.broadcasted_iota(jnp.int32, value.shape, 0)
        col = lax.broadcasted_iota(jnp.int32, value.shape, 1) + 256 * n
        return COEF_TWO * gram + COEF_THREE * value + jnp.where(row == col, COEF_ONE, 0.0)

    now, later = (xh, xl), (vh, vl)
    for sweep in range(SWEEPS):
        symmetric(yh, yl, now[0], now[1], gh, gl, lambda value, n: value)
        symmetric(gh, gl, gh, gl, wh, wl, polynomial)
        for n in range(3):
            value = product(now[0][...], now[1][...], wh, wl, tile(n))
            if sweep == SWEEPS - 1:
                value = value * math.sqrt(K)
                x[:, tile(n)] = value
            later[0][:, tile(n)], later[1][:, tile(n)] = halves(value)
            yh[tile(n), :], yl[tile(n), :] = halves(value.T)
        now, later = later, now

    my_rows = pl.ds(pl.multiple_of(r * SLAB, SLAB), SLAB)
    iso_ref[...] = x[my_rows, :]
    for rr, hh, sem in ((ring_left, 1, 1), (ring_right, 0, 3), (ring_far, 0, 4), (ring_far, 1, 5)):
        wait(slab_half(rr, hh), c3_recv.at[sem])
    split(cf, gh, gl, K, 64)

    for n in range(3):
        uh[:, tile(n)], ul[:, tile(n)] = halves(product(yh[my_rows, :], yl[my_rows, :], gh, gl, tile(n)))
    for n in range(3):
        env_ref[:, tile(n)] = product(uh[...], ul[...], now[0], now[1], tile(n))

    for f in range(3):
        gather_sent(f)
    to_owners_sent(c1_send)

    @pl.when(is_owner)
    def _():
        wait(co.at[pl.ds(0, 63)], c2_send)

    wait(cf.at[pl.ds(0, 3 * SLAB)], c3_send)


def body(amplitudes, left_terms, right_terms, source_list, list_count, weight_index, weight_table):
    vmem = pl.BlockSpec(memory_space=pltpu.VMEM)
    smem = pl.BlockSpec(memory_space=pltpu.SMEM)
    dma = pltpu.SemaphoreType.DMA
    slab = jax.ShapeDtypeStruct((SLAB, K), F32)
    iso, env = pl.pallas_call(
        kernel,
        out_shape=(slab, slab),
        in_specs=[vmem] + [pl.BlockSpec(memory_space=pl.ANY)] * 2 + [smem] * 4,
        out_specs=(vmem, vmem),
        scratch_shapes=[
            pltpu.VMEM((SLAB, K), BF), pltpu.VMEM((SLAB, K), BF),
            *[pltpu.VMEM((K, K), BF)] * 12,
            pltpu.VMEM((SLAB, K), BF), pltpu.VMEM((SLAB, K), BF),
            pltpu.VMEM((SLAB, K), F32),
            pltpu.VMEM((K, K), F32), pltpu.VMEM((K, K), F32), pltpu.VMEM((2, 96, K), F32),
            pltpu.VMEM((3, 2, 16, 6, TR, TC), F32),
            pltpu.VMEM((2, 32, TR, TC), F32),
            pltpu.VMEM((3, TR, TC), F32),
            pltpu.VMEM((64, TR, TC), F32),
            pltpu.VMEM((64, TR, TC), F32),
            pltpu.VMEM((K, K), F32),
            pltpu.VMEM((SLAB, K), F32),
            dma((2,)),
            dma((3,)), dma((3, 6)), dma((3,)), dma((3, 3)), dma((3,)), dma((3, 12)), dma((3,)), dma((3, 16)),
            dma((2,)), dma((2, 3)), dma((2,)), dma((2,)), dma, dma, dma, dma, dma, dma((6,)),
        ],
        compiler_params=pltpu.CompilerParams(
            collective_id=0, has_side_effects=True, vmem_limit_bytes=56 * 1024 * 1024
        ),
        cost_estimate=pl.CostEstimate(flops=28 * 10**9, bytes_accessed=8 * 10**6, transcendentals=0),
    )(
        amplitudes, left_terms.reshape(SLAB, K), right_terms.reshape(K, K),
        source_list.T, list_count, weight_index.T, weight_table,
    )
    return iso, env.reshape(1, SLAB, K)


def solution(mesh):
    placed = (P("rows", None), P("terms", "rows", None), P("terms", None, None), P(), P(), P(), P())
    return jax.shard_map(
        body,
        mesh=mesh,
        in_specs=placed,
        out_specs=(P("rows", None), P("terms", "rows", None)),
        check_vma=False,
    )
```

```python
import math

import jax
import jax.numpy as jnp
from jax import lax
from jax.experimental import pallas as pl
from jax.experimental.pallas import tpu as pltpu
from jax.sharding import PartitionSpec as P

K = 768
FAN = 4
SWEEPS = 3
SLAB = 192
OWNERS = 48
TR, TC = 8, 384
COEF_ONE = 3.4445
COEF_TWO = -4.775
COEF_THREE = 2.0315
MESH = pl.DeviceIdType.MESH
BF = jnp.bfloat16
F32 = jnp.float32


def halves(value):
    high = value.astype(BF)
    return high, (value - high.astype(F32)).astype(BF)


def split(src, high, low, rows, step):
    @pl.loop(0, rows // step)
    def _(i):
        at = pl.ds(pl.multiple_of(i * step, step), step)
        high[at, :], low[at, :] = halves(src[at, :])


def product(ah, al, bh, bl, cols):
    rows = ah.shape[0]
    right = bh[:, cols]
    both = jnp.dot(jnp.concatenate([ah, al], axis=0), right, preferred_element_type=F32)
    return both[:rows] + (both[rows:] + jnp.dot(ah, bl[:, cols], preferred_element_type=F32))


def wait(ref, sem):
    pltpu.make_async_copy(ref, ref, sem).wait()


def kernel(
    a_ref, l_hbm, r_hbm, source, count, windex, wtable,
    iso_ref, env_ref,
    lh, ll, rh, rl, xh, xl, vh, vl, yh, yl, gh, gl, wh, wl, uh, ul, part, x, w, pre,
    ga, rs, mine, cb, co, cf, l_ref, in_sem,
    z_send, z_recv, s1_send, s1_recv, s2_send, s2_recv, sib_send, sib_recv,
    pre_send, pre_recv, rs_send, rs_recv, c1_send, c1_recv, c2_send, c2_recv, c3_send, c3_recv,
):
    t = lax.axis_index("terms")
    r = lax.axis_index("rows")
    core = t % 2
    cy = (t // 2) % 4
    zl = (t // 8) % 2
    cx = t // 16
    pos = cx * 4 + cy
    dq = zl * 2 + core
    q = jnp.where(pos % 2 == 1, 3 - dq, dq)
    is_owner = q < 3
    own = jnp.minimum(pos * 3 + q, OWNERS - 1)

    def term(xx, zz, yy, cc):
        return ((xx * 2 + zz) * 4 + yy) * 2 + cc

    def owner_term(m):
        p = m // 3
        qq = m % 3
        d = jnp.where(p % 2 == 1, 3 - qq, qq)
        return term(p // 4, d // 2, p % 4, d % 2)

    def chunk(ref, m, row0=0):
        rows = pl.ds(pl.multiple_of(row0 + (m // 2) * TR, TR), TR)
        return ref.at[rows, pl.ds(pl.multiple_of((m % 2) * TC, TC), TC)]

    def there(tt, rr):
        return {"terms": tt, "rows": rr}

    def remote(src, dst, send, recv, tt, rr):
        return pltpu.make_async_remote_copy(
            src_ref=src, dst_ref=dst, send_sem=send, recv_sem=recv,
            device_id=there(tt, rr), device_id_type=MESH,
        )

    bring_l = pltpu.make_async_copy(l_hbm, l_ref, in_sem.at[0])
    bring_r = pltpu.make_async_copy(r_hbm, w, in_sem.at[1])
    bring_l.start()
    bring_r.start()
    barrier = pltpu.get_barrier_semaphore()

    @pl.loop(1, 64)
    def _(i):
        pl.semaphore_signal(barrier, inc=1, device_id=there((t + i) % 64, r), device_id_type=MESH)

    for dr in range(1, 4):
        for zz in range(2):
            for cc in range(2):
                pl.semaphore_signal(
                    barrier, inc=1, device_id=there(term(cx, zz, cy, cc), (r + dr) % 4), device_id_type=MESH
                )
    bring_l.wait()
    split(l_ref, lh, ll, SLAB, 48)
    bring_r.wait()
    split(w, rh, rl, K, 64)
    pl.semaphore_wait(barrier, 75)

    def to_owners(src, dst, send, recv):
        @pl.loop(0, OWNERS)
        def _(i):
            m = (i + own) % OWNERS
            o = owner_term(m)
            slot = (t - o + 63) % 64

            @pl.when(o != t)
            def _():
                remote(chunk(src, m), dst.at[slot], send, recv, o, r).start()

        @pl.when(is_owner)
        def _():
            dst[63] = chunk(src, own)[...]

    def to_owners_sent(send):
        @pl.when(is_owner)
        def _():
            wait(cb.at[pl.ds(0, 47)], send)

        @pl.when(jnp.logical_not(is_owner))
        def _():
            wait(cb.at[pl.ds(0, 48)], send)

    sibling = term(cx, zl, cy, 1 - core)
    kept = pl.ds(pl.multiple_of(core * 96, 96), 96)
    given = pl.ds(pl.multiple_of((1 - core) * 96, 96), 96)
    keeps_own = jnp.logical_and(is_owner, own // 24 == core)

    def tile(n):
        return pl.ds(n * 256, 256)

    def pre_start(f, n):
        remote(part.at[given, tile(n)], pre.at[f, :, tile(n)], pre_send.at[f], pre_recv.at[f, n], sibling, r).start()

    def pre_add(f, n):
        wait(pre.at[f, :, tile(n)], pre_recv.at[f, n])
        part[kept, tile(n)] = part[kept, tile(n)] + pre[f, :, tile(n)]

    def reduce_start(f, side):
        @pl.loop(0, 12)
        def _(i):
            m = 24 * core + 2 * ((i + pos) % 12) + side
            o = owner_term(m)
            dst = rs.at[f, (t // 2 - o // 2 + 31) % 32]

            @pl.when(o != t)
            def _():
                remote(chunk(part, m), dst, rs_send.at[f], rs_recv.at[f], o, r).start()

            @pl.when(o == t)
            def _():
                pltpu.make_async_copy(chunk(part, m), dst, rs_recv.at[f]).start()

    def reduce_sent(f):
        wait(pre.at[f], pre_send.at[f])

        @pl.when(keeps_own)
        def _():
            wait(rs.at[f, pl.ds(0, 23)], rs_send.at[f])

        @pl.when(jnp.logical_not(keeps_own))
        def _():
            wait(rs.at[f, pl.ds(0, 24)], rs_send.at[f])

    side_b = jnp.where(core == 0, cx, cy)
    side_a = jnp.where(core == 0, cy, cx)
    here = side_b * 4 + side_a
    kk = 4 * jnp.minimum(q, 2) + r
    to_core = kk // 6
    to_slot = kk % 6
    to_pos = jnp.where(to_core == 0, cx * 4 + cy, cy * 4 + cx)

    def partner(bb, aa):
        return term(jnp.where(core == 0, bb, aa), zl, jnp.where(core == 0, aa, bb), core)

    def gather_start(f):
        @pl.when(is_owner)
        def _():
            for dr in (2, 1, 3, 0):
                for dz in (1, 0):
                    tt, rr = term(cx, (zl + dz) % 2, cy, to_core), (r + dr) % 4
                    dst = ga.at[f, to_core, to_pos, to_slot]
                    if dz == 0 and dr == 0:
                        @pl.when(to_core == core)
                        def _():
                            pltpu.make_async_copy(mine.at[f], dst, z_recv.at[f, to_slot]).start()

                        @pl.when(to_core != core)
                        def _():
                            remote(mine.at[f], dst, z_send.at[f], z_recv.at[f, to_slot], tt, rr).start()
                    else:
                        remote(mine.at[f], dst, z_send.at[f], z_recv.at[f, to_slot], tt, rr).start()

    def gather_rest(f, after_z=None, after_push=None):
        for i in range(6):
            wait(ga.at[f, core, here, i], z_recv.at[f, i])

        def block(bb, d):
            return ga.at[f, core, bb * 4 + (side_a + 4 - d) % 4]

        def across(bb, d, sem):
            remote(block(bb, d), block(bb, d), sib_send.at[f], sib_recv.at[f, sem], sibling, r).start()

        def push(bb, d, tt, sem):
            remote(block(bb, d), block(bb, d), s2_send.at[f], s2_recv.at[f, sem], tt, r).start()

        mine_now = block(side_b, 0)
        for d in (1, 3, 2):
            remote(mine_now, mine_now, s1_send.at[f], s1_recv.at[f, d - 1], partner(side_b, (side_a + d) % 4), r).start()
        if after_z:
            after_z()
        order = (0, 1, 3, 2)
        for d in order:
            if d > 0:
                wait(block(side_b, d), s1_recv.at[f, d - 1])
            for n in (1, 3) if d in (0, 1) else (1, 3, 2):
                push(side_b, d, partner((side_b + n) % 4, side_a), 4 * (n - 1) + d)
            across(side_b, d, d)
        if after_push:
            after_push()
        for n, d in [(n, d) for d in order for n in (1, 3)] + [(2, d) for d in (0, 1, 3, 2)]:
            bb = (side_b + 4 - n) % 4
            wait(block(bb, d), s2_recv.at[f, 4 * (n - 1) + d])
            if (n, d) in ((1, 0), (3, 1)):
                push(bb, d, partner((side_b + n) % 4, side_a), 4 + d)
            across(bb, d, 4 * n + d)
        for n in (0, 1, 3, 2):
            for d in order:
                bb = (side_a + 4 - n) % 4
                wait(ga.at[f, 1 - core, bb * 4 + (side_b + 4 - d) % 4], sib_recv.at[f, 4 * n + d])

    def gather_sent(f):
        @pl.when(is_owner)
        def _():
            @pl.when(to_core == core)
            def _():
                wait(cb.at[pl.ds(0, 7)], z_send.at[f])

            @pl.when(to_core != core)
            def _():
                wait(cb.at[pl.ds(0, 8)], z_send.at[f])

        wait(ga.at[f, 0, pl.ds(0, 3)], s1_send.at[f])
        wait(ga.at[f, 0, pl.ds(0, 12)], s2_send.at[f])
        wait(ga.at[f, 0], sib_send.at[f])

    def assemble(f):
        for cc in range(2):
            @pl.loop(0, 16)
            def _(s):
                p = s if cc == 0 else (s % 4) * 4 + s // 4
                for i in range(6):
                    k = 6 * cc + i
                    m = p * 3 + k // 4
                    chunk(x, m, (k % 4) * SLAB)[...] = ga[f, cc, s, i]

    def apply_terms(f):
        split(x, xh, xl, K, 64)

        @pl.loop(0, 3)
        def _(n):
            cols = pl.ds(pl.multiple_of(n * 256, 256), 256)
            uh[:, cols], ul[:, cols] = halves(product(lh[...], ll[...], xh, xl, cols))

        for n in range(3):
            part[:, tile(n)] = product(uh[...], ul[...], rh, rl, tile(n))
            pre_start(f, n)
        pre_add(f, 0)
        pre_add(f, 1)
        reduce_start(f, 0)
        pre_add(f, 2)
        reduce_start(f, 1)

    @pl.when(is_owner)
    def _():
        mine[0] = chunk(a_ref, own)[...]

    gather_start(0)
    to_owners(l_ref, cb, c1_send, c1_recv)
    gather_rest(0)

    ring_right, ring_left, ring_far = (r + 1) % 4, (r + 3) % 4, (r + 2) % 4

    def slab_half(rr, hh):
        return cf.at[pl.ds(pl.multiple_of(rr * SLAB + hh * 96, 96), 96)]

    def go_round(rr, hh, to, sem):
        remote(slab_half(rr, hh), slab_half(rr, hh), c3_send, c3_recv.at[sem], t, to).start()

    def mix():
        @pl.when(is_owner)
        def _():
            wait(cb.at[pl.ds(0, 63)], c1_recv)

            @pl.loop(0, 64)
            def _(j):
                total = jnp.zeros((TR, TC), F32)
                for c in range(FAN):
                    weight = jnp.where(c < count[j], wtable[windex[c, j]], 0.0)
                    total = total + weight * cb[(source[c, j] - t + 63) % 64]
                co[j] = total

    def give_back():
        @pl.when(is_owner)
        def _():
            dst = chunk(cf, own, r * SLAB)

            @pl.loop(1, 64)
            def _(i):
                j = (i + t) % 64
                remote(co.at[j], dst, c2_send, c2_recv, j, r).start()

            pltpu.make_async_copy(co.at[t], dst, c2_recv).start()

    def first_round():
        wait(cf.at[pl.ds(pl.multiple_of(r * SLAB, SLAB), SLAB)], c2_recv)
        go_round(r, 0, ring_right, 0)
        go_round(r, 1, ring_left, 2)

    def second_round():
        go_round(r, 1, ring_right, 1)
        go_round(r, 0, ring_left, 3)
        wait(slab_half(ring_left, 0), c3_recv.at[0])
        go_round(ring_left, 0, ring_right, 4)
        wait(slab_half(ring_right, 1), c3_recv.at[2])
        go_round(ring_right, 1, ring_left, 5)

    for f in range(2):
        assemble(f)
        apply_terms(f)
        if f == 0:
            mix()

        @pl.when(is_owner)
        def _():
            wait(rs.at[f], rs_recv.at[f])
            mine[f + 1] = mine[f] - 0.3 * jnp.sum(rs[f], axis=0)

        gather_start(f + 1)
        if f == 0:
            give_back()
        reduce_sent(f)
        if f == 0:
            gather_rest(1, after_push=first_round)
        else:
            gather_rest(2, after_z=second_round)

    assemble(2)
    squares = jnp.sum(lax.fori_loop(
        0, 12,
        lambda i, s: s + jnp.sum((x[pl.ds(pl.multiple_of(i * 64, 64), 64), :] ** 2).reshape(8, 8, K), axis=0),
        jnp.zeros((8, K), F32),
    ))
    scale = 1.0 / jnp.sqrt(jnp.full((8, 128), squares, F32))[0:1, 0:1]
    for n in range(3):
        value = x[tile(n), :] * scale
        xh[tile(n), :], xl[tile(n), :] = halves(value)
        yh[:, tile(n)], yl[:, tile(n)] = halves(value.T)

    def symmetric(ah, al, bh, bl, oh, ol, last):
        for n in range(3):
            top = 256 * (n + 1)
            value = last(product(ah[:top, :], al[:top, :], bh, bl, tile(n)), n)
            oh[:top, tile(n)], ol[:top, tile(n)] = halves(value)
            for m in range(n):
                oh[tile(n), tile(m)], ol[tile(n), tile(m)] = halves(value[256 * m:256 * (m + 1)].T)

    def polynomial(value, n):
        top = value.shape[0]
        gram = gh[:top, tile(n)].astype(F32) + gl[:top, tile(n)].astype(F32)
        row = lax.broadcasted_iota(jnp.int32, value.shape, 0)
        col = lax.broadcasted_iota(jnp.int32, value.shape, 1) + 256 * n
        return COEF_TWO * gram + COEF_THREE * value + jnp.where(row == col, COEF_ONE, 0.0)

    now, later = (xh, xl), (vh, vl)
    for sweep in range(SWEEPS):
        symmetric(yh, yl, now[0], now[1], gh, gl, lambda value, n: value)
        symmetric(gh, gl, gh, gl, wh, wl, polynomial)
        for n in range(3):
            value = product(now[0][...], now[1][...], wh, wl, tile(n))
            if sweep == SWEEPS - 1:
                value = value * math.sqrt(K)
                x[:, tile(n)] = value
            later[0][:, tile(n)], later[1][:, tile(n)] = halves(value)
            yh[tile(n), :], yl[tile(n), :] = halves(value.T)
        now, later = later, now

    my_rows = pl.ds(pl.multiple_of(r * SLAB, SLAB), SLAB)
    iso_ref[...] = x[my_rows, :]
    for rr, hh, sem in ((ring_left, 1, 1), (ring_right, 0, 3), (ring_far, 0, 4), (ring_far, 1, 5)):
        wait(slab_half(rr, hh), c3_recv.at[sem])
    split(cf, gh, gl, K, 64)

    for n in range(3):
        uh[:, tile(n)], ul[:, tile(n)] = halves(product(yh[my_rows, :], yl[my_rows, :], gh, gl, tile(n)))
    for n in range(3):
        env_ref[:, tile(n)] = product(uh[...], ul[...], now[0], now[1], tile(n))

    for f in range(3):
        gather_sent(f)
    to_owners_sent(c1_send)

    @pl.when(is_owner)
    def _():
        wait(co.at[pl.ds(0, 63)], c2_send)

    wait(cf.at[pl.ds(0, 3 * SLAB)], c3_send)


def hand_on(iso_in, env_in, iso_out, env_out, sem):
    copies = [
        pltpu.make_async_copy(iso_in, iso_out, sem.at[0]),
        pltpu.make_async_copy(env_in, env_out, sem.at[1]),
    ]
    for copy in copies:
        copy.start()
    for copy in copies:
        copy.wait()


def body(amplitudes, left_terms, right_terms, source_list, list_count, weight_index, weight_table):
    vmem = pl.BlockSpec(memory_space=pltpu.VMEM)
    smem = pl.BlockSpec(memory_space=pltpu.SMEM)
    dma = pltpu.SemaphoreType.DMA
    slab = jax.ShapeDtypeStruct((SLAB, K), F32)
    iso, env = pl.pallas_call(
        kernel,
        out_shape=(slab, slab),
        in_specs=[vmem] + [pl.BlockSpec(memory_space=pl.ANY)] * 2 + [smem] * 4,
        out_specs=(vmem, vmem),
        scratch_shapes=[
            pltpu.VMEM((SLAB, K), BF), pltpu.VMEM((SLAB, K), BF),
            *[pltpu.VMEM((K, K), BF)] * 12,
            pltpu.VMEM((SLAB, K), BF), pltpu.VMEM((SLAB, K), BF),
            pltpu.VMEM((SLAB, K), F32),
            pltpu.VMEM((K, K), F32), pltpu.VMEM((K, K), F32), pltpu.VMEM((2, 96, K), F32),
            pltpu.VMEM((3, 2, 16, 6, TR, TC), F32),
            pltpu.VMEM((2, 32, TR, TC), F32),
            pltpu.VMEM((3, TR, TC), F32),
            pltpu.VMEM((64, TR, TC), F32),
            pltpu.VMEM((64, TR, TC), F32),
            pltpu.VMEM((K, K), F32),
            pltpu.VMEM((SLAB, K), F32),
            dma((2,)),
            dma((3,)), dma((3, 6)), dma((3,)), dma((3, 3)), dma((3,)), dma((3, 12)), dma((3,)), dma((3, 16)),
            dma((2,)), dma((2, 3)), dma((2,)), dma((2,)), dma, dma, dma, dma, dma, dma((6,)),
        ],
        compiler_params=pltpu.CompilerParams(
            collective_id=0, has_side_effects=True, vmem_limit_bytes=56 * 1024 * 1024
        ),
        cost_estimate=pl.CostEstimate(flops=28 * 10**9, bytes_accessed=8 * 10**6, transcendentals=0),
    )(
        amplitudes, left_terms.reshape(SLAB, K), right_terms.reshape(K, K),
        source_list.T, list_count, weight_index.T, weight_table,
    )
    anywhere = pl.BlockSpec(memory_space=pl.ANY)
    iso, env = pl.pallas_call(
        hand_on,
        out_shape=(slab, slab),
        in_specs=[anywhere] * 2,
        out_specs=(anywhere,) * 2,
        scratch_shapes=[dma((2,))],
        cost_estimate=pl.CostEstimate(flops=0, bytes_accessed=4 * SLAB * K * 4, transcendentals=0),
    )(iso, env)
    return iso, env.reshape(1, SLAB, K)


def solution(mesh):
    placed = (P("rows", None), P("terms", "rows", None), P("terms", None, None), P(), P(), P(), P())
    return jax.shard_map(
        body,
        mesh=mesh,
        in_specs=placed,
        out_specs=(P("rows", None), P("terms", "rows", None)),
        check_vma=False,
    )
```

```python
import math

import jax
import jax.numpy as jnp
from jax import lax
from jax.experimental import pallas as pl
from jax.experimental.pallas import tpu as pltpu
from jax.sharding import PartitionSpec as P

K = 768
FAN = 4
SWEEPS = 3
SLAB = 192
OWNERS = 48
TR, TC = 8, 384
COEF_ONE = 3.4445
COEF_TWO = -4.775
COEF_THREE = 2.0315
MESH = pl.DeviceIdType.MESH
BF = jnp.bfloat16
F32 = jnp.float32


def halves(value):
    high = value.astype(BF)
    return high, (value - high.astype(F32)).astype(BF)


def split(src, high, low, rows, step):
    @pl.loop(0, rows // step)
    def _(i):
        at = pl.ds(pl.multiple_of(i * step, step), step)
        high[at, :], low[at, :] = halves(src[at, :])


def product(ah, al, bh, bl, cols):
    return joined(ah, al, bh[:, cols], bl[:, cols])


def joined(ah, al, bh, bl):
    rows = ah.shape[0]
    both = jnp.dot(jnp.concatenate([ah, al], axis=0), bh, preferred_element_type=F32)
    return both[:rows] + (both[rows:] + jnp.dot(ah, bl, preferred_element_type=F32))


def wait(ref, sem):
    pltpu.make_async_copy(ref, ref, sem).wait()


def kernel(
    a_ref, l_hbm, r_hbm, source, count, windex, wtable,
    iso_ref, env_ref,
    lh, ll, rh, rl, xh, xl, vh, vl, yh, yl, gh, gl, wh, wl, uh, ul, part, x, w, pre,
    ga, rs, mine, cb, co, cf, l_ref, in_sem,
    z_send, z_recv, s1_send, s1_recv, s2_send, s2_recv, sib_send, sib_recv,
    pre_send, pre_recv, rs_send, rs_recv, c1_send, c1_recv, c2_send, c2_recv, c3_send, c3_recv,
):
    t = lax.axis_index("terms")
    r = lax.axis_index("rows")
    core = t % 2
    cy = (t // 2) % 4
    zl = (t // 8) % 2
    cx = t // 16
    pos = cx * 4 + cy
    dq = zl * 2 + core
    q = jnp.where(pos % 2 == 1, 3 - dq, dq)
    is_owner = q < 3
    own = jnp.minimum(pos * 3 + q, OWNERS - 1)

    def term(xx, zz, yy, cc):
        return ((xx * 2 + zz) * 4 + yy) * 2 + cc

    def owner_term(m):
        p = m // 3
        qq = m % 3
        d = jnp.where(p % 2 == 1, 3 - qq, qq)
        return term(p // 4, d // 2, p % 4, d % 2)

    def chunk(ref, m, row0=0):
        rows = pl.ds(pl.multiple_of(row0 + (m // 2) * TR, TR), TR)
        return ref.at[rows, pl.ds(pl.multiple_of((m % 2) * TC, TC), TC)]

    def there(tt, rr):
        return {"terms": tt, "rows": rr}

    def remote(src, dst, send, recv, tt, rr):
        return pltpu.make_async_remote_copy(
            src_ref=src, dst_ref=dst, send_sem=send, recv_sem=recv,
            device_id=there(tt, rr), device_id_type=MESH,
        )

    bring_l = pltpu.make_async_copy(l_hbm, l_ref, in_sem.at[0])
    bring_r = pltpu.make_async_copy(r_hbm, w, in_sem.at[1])
    bring_l.start()
    bring_r.start()
    barrier = pltpu.get_barrier_semaphore()

    for dr in (2, 1, 3):
        for zz in range(2):
            for cc in range(2):
                pl.semaphore_signal(
                    barrier, inc=1, device_id=there(term(cx, zz, cy, cc), (r + dr) % 4), device_id_type=MESH
                )

    @pl.loop(1, 64)
    def _(i):
        pl.semaphore_signal(barrier, inc=1, device_id=there((t + i) % 64, r), device_id_type=MESH)

    bring_l.wait()
    split(l_ref, lh, ll, SLAB, 48)
    bring_r.wait()
    split(w, rh, rl, K, 64)
    pl.semaphore_wait(barrier, 75)

    def to_owners(src, dst, send, recv):
        @pl.loop(0, OWNERS)
        def _(i):
            m = (i + own) % OWNERS
            o = owner_term(m)
            slot = (t - o + 63) % 64

            @pl.when(o != t)
            def _():
                remote(chunk(src, m), dst.at[slot], send, recv, o, r).start()

        @pl.when(is_owner)
        def _():
            dst[63] = chunk(src, own)[...]

    def to_owners_sent(send):
        @pl.when(is_owner)
        def _():
            wait(cb.at[pl.ds(0, 47)], send)

        @pl.when(jnp.logical_not(is_owner))
        def _():
            wait(cb.at[pl.ds(0, 48)], send)

    sibling = term(cx, zl, cy, 1 - core)
    kept = pl.ds(pl.multiple_of(core * 96, 96), 96)
    given = pl.ds(pl.multiple_of((1 - core) * 96, 96), 96)
    keeps_own = jnp.logical_and(is_owner, own // 24 == core)

    def tile(n):
        return pl.ds(n * 256, 256)

    def pre_start(f, n):
        remote(part.at[given, tile(n)], pre.at[f, :, tile(n)], pre_send.at[f], pre_recv.at[f, n], sibling, r).start()

    def pre_add(f, n):
        wait(pre.at[f, :, tile(n)], pre_recv.at[f, n])
        part[kept, tile(n)] = part[kept, tile(n)] + pre[f, :, tile(n)]

    def reduce_start(f, side):
        @pl.loop(0, 12)
        def _(i):
            m = 24 * core + 2 * ((i + pos) % 12) + side
            o = owner_term(m)
            dst = rs.at[f, (t // 2 - o // 2 + 31) % 32]

            @pl.when(o != t)
            def _():
                remote(chunk(part, m), dst, rs_send.at[f], rs_recv.at[f], o, r).start()

            @pl.when(o == t)
            def _():
                pltpu.make_async_copy(chunk(part, m), dst, rs_recv.at[f]).start()

    def reduce_sent(f):
        wait(pre.at[f], pre_send.at[f])

        @pl.when(keeps_own)
        def _():
            wait(rs.at[f, pl.ds(0, 23)], rs_send.at[f])

        @pl.when(jnp.logical_not(keeps_own))
        def _():
            wait(rs.at[f, pl.ds(0, 24)], rs_send.at[f])

    side_b = jnp.where(core == 0, cx, cy)
    side_a = jnp.where(core == 0, cy, cx)
    here = side_b * 4 + side_a
    kk = 4 * jnp.minimum(q, 2) + r
    to_core = kk // 6
    to_slot = kk % 6
    to_pos = jnp.where(to_core == 0, cx * 4 + cy, cy * 4 + cx)

    def partner(bb, aa):
        return term(jnp.where(core == 0, bb, aa), zl, jnp.where(core == 0, aa, bb), core)

    def gather_start(f):
        @pl.when(is_owner)
        def _():
            for dr in (2, 1, 3, 0):
                for dz in (1, 0):
                    tt, rr = term(cx, (zl + dz) % 2, cy, to_core), (r + dr) % 4
                    dst = ga.at[f, to_core, to_pos, to_slot]
                    if dz == 0 and dr == 0:
                        @pl.when(to_core == core)
                        def _():
                            pltpu.make_async_copy(mine.at[f], dst, z_recv.at[f, to_slot]).start()

                        @pl.when(to_core != core)
                        def _():
                            remote(mine.at[f], dst, z_send.at[f], z_recv.at[f, to_slot], tt, rr).start()
                    else:
                        remote(mine.at[f], dst, z_send.at[f], z_recv.at[f, to_slot], tt, rr).start()

    def gather_rest(f, after_z=None, after_push=None):
        for i in range(6):
            wait(ga.at[f, core, here, i], z_recv.at[f, i])

        def block(bb, d):
            return ga.at[f, core, bb * 4 + (side_a + 4 - d) % 4]

        def across(bb, d, sem):
            remote(block(bb, d), block(bb, d), sib_send.at[f], sib_recv.at[f, sem], sibling, r).start()

        def push(bb, d, tt, sem):
            remote(block(bb, d), block(bb, d), s2_send.at[f], s2_recv.at[f, sem], tt, r).start()

        mine_now = block(side_b, 0)
        for d in (1, 3, 2):
            remote(mine_now, mine_now, s1_send.at[f], s1_recv.at[f, d - 1], partner(side_b, (side_a + d) % 4), r).start()
        if after_z:
            after_z()
        order = (0, 1, 3, 2)
        for d in order:
            if d > 0:
                wait(block(side_b, d), s1_recv.at[f, d - 1])
            for n in (1, 3) if d in (0, 1) else (1, 3, 2):
                push(side_b, d, partner((side_b + n) % 4, side_a), 4 * (n - 1) + d)
            across(side_b, d, d)
        if after_push:
            after_push()
        for n, d in [(n, d) for d in order for n in (1, 3)] + [(2, d) for d in (0, 1, 3, 2)]:
            bb = (side_b + 4 - n) % 4
            wait(block(bb, d), s2_recv.at[f, 4 * (n - 1) + d])
            if (n, d) in ((1, 0), (3, 1)):
                push(bb, d, partner((side_b + n) % 4, side_a), 4 + d)
            across(bb, d, 4 * n + d)
        for n in (0, 1, 3, 2):
            for d in order:
                bb = (side_a + 4 - n) % 4
                wait(ga.at[f, 1 - core, bb * 4 + (side_b + 4 - d) % 4], sib_recv.at[f, 4 * n + d])

    def gather_sent(f):
        @pl.when(is_owner)
        def _():
            @pl.when(to_core == core)
            def _():
                wait(cb.at[pl.ds(0, 7)], z_send.at[f])

            @pl.when(to_core != core)
            def _():
                wait(cb.at[pl.ds(0, 8)], z_send.at[f])

        wait(ga.at[f, 0, pl.ds(0, 3)], s1_send.at[f])
        wait(ga.at[f, 0, pl.ds(0, 12)], s2_send.at[f])
        wait(ga.at[f, 0], sib_send.at[f])

    def assemble(f):
        for cc in range(2):
            @pl.loop(0, 16)
            def _(s):
                p = s if cc == 0 else (s % 4) * 4 + s // 4
                for i in range(6):
                    k = 6 * cc + i
                    m = p * 3 + k // 4
                    chunk(x, m, (k % 4) * SLAB)[...] = ga[f, cc, s, i]

    def apply_terms(f):
        for n in range(3):
            high, low = halves(x[:, tile(n)])
            uh[:, tile(n)], ul[:, tile(n)] = halves(joined(lh[...], ll[...], high, low))

        for n in range(3):
            part[:, tile(n)] = product(uh[...], ul[...], rh, rl, tile(n))
            pre_start(f, n)
        pre_add(f, 0)
        pre_add(f, 1)
        reduce_start(f, 0)
        pre_add(f, 2)
        reduce_start(f, 1)

    @pl.when(is_owner)
    def _():
        mine[0] = chunk(a_ref, own)[...]

    gather_start(0)
    to_owners(l_ref, cb, c1_send, c1_recv)
    gather_rest(0)

    ring_right, ring_left, ring_far = (r + 1) % 4, (r + 3) % 4, (r + 2) % 4

    def slab_half(rr, hh):
        return cf.at[pl.ds(pl.multiple_of(rr * SLAB + hh * 96, 96), 96)]

    def go_round(rr, hh, to, sem):
        remote(slab_half(rr, hh), slab_half(rr, hh), c3_send, c3_recv.at[sem], t, to).start()

    def mix():
        @pl.when(is_owner)
        def _():
            wait(cb.at[pl.ds(0, 63)], c1_recv)

            @pl.loop(0, 64)
            def _(j):
                total = jnp.zeros((TR, TC), F32)
                for c in range(FAN):
                    weight = jnp.where(c < count[j], wtable[windex[c, j]], 0.0)
                    total = total + weight * cb[(source[c, j] - t + 63) % 64]
                co[j] = total

    def give_back():
        @pl.when(is_owner)
        def _():
            dst = chunk(cf, own, r * SLAB)

            @pl.loop(1, 64)
            def _(i):
                j = (i + t) % 64
                remote(co.at[j], dst, c2_send, c2_recv, j, r).start()

            pltpu.make_async_copy(co.at[t], dst, c2_recv).start()

    def first_round():
        wait(cf.at[pl.ds(pl.multiple_of(r * SLAB, SLAB), SLAB)], c2_recv)
        go_round(r, 0, ring_right, 0)
        go_round(r, 1, ring_left, 2)

    def second_round():
        go_round(r, 1, ring_right, 1)
        go_round(r, 0, ring_left, 3)
        wait(slab_half(ring_left, 0), c3_recv.at[0])
        go_round(ring_left, 0, ring_right, 4)
        wait(slab_half(ring_right, 1), c3_recv.at[2])
        go_round(ring_right, 1, ring_left, 5)

    for f in range(2):
        assemble(f)
        apply_terms(f)
        if f == 0:
            mix()

        @pl.when(is_owner)
        def _():
            wait(rs.at[f], rs_recv.at[f])
            mine[f + 1] = mine[f] - 0.3 * jnp.sum(rs[f], axis=0)

        gather_start(f + 1)
        if f == 0:
            give_back()
        reduce_sent(f)
        if f == 0:
            gather_rest(1, after_push=first_round)
        else:
            gather_rest(2, after_z=second_round)

    assemble(2)
    squares = jnp.sum(lax.fori_loop(
        0, 12,
        lambda i, s: s + jnp.sum((x[pl.ds(pl.multiple_of(i * 64, 64), 64), :] ** 2).reshape(8, 8, K), axis=0),
        jnp.zeros((8, K), F32),
    ))
    scale = 1.0 / jnp.sqrt(jnp.full((8, 128), squares, F32))[0:1, 0:1]
    for n in range(3):
        value = x[tile(n), :] * scale
        xh[tile(n), :], xl[tile(n), :] = halves(value)
        yh[:, tile(n)], yl[:, tile(n)] = halves(value.T)

    def symmetric(ah, al, bh, bl, oh, ol, last):
        for n in range(3):
            top = 256 * (n + 1)
            value = last(product(ah[:top, :], al[:top, :], bh, bl, tile(n)), n)
            oh[:top, tile(n)], ol[:top, tile(n)] = halves(value)
            for m in range(n):
                oh[tile(n), tile(m)], ol[tile(n), tile(m)] = halves(value[256 * m:256 * (m + 1)].T)

    def polynomial(value, n):
        top = value.shape[0]
        gram = gh[:top, tile(n)].astype(F32) + gl[:top, tile(n)].astype(F32)
        row = lax.broadcasted_iota(jnp.int32, value.shape, 0)
        col = lax.broadcasted_iota(jnp.int32, value.shape, 1) + 256 * n
        return COEF_TWO * gram + COEF_THREE * value + jnp.where(row == col, COEF_ONE, 0.0)

    now, later = (xh, xl), (vh, vl)
    for sweep in range(SWEEPS):
        symmetric(yh, yl, now[0], now[1], gh, gl, lambda value, n: value)
        symmetric(gh, gl, gh, gl, wh, wl, polynomial)
        if sweep == SWEEPS - 1:
            for rr, hh, sem in ((ring_left, 1, 1), (ring_right, 0, 3), (ring_far, 0, 4), (ring_far, 1, 5)):
                wait(slab_half(rr, hh), c3_recv.at[sem])
        for n in range(3):
            value = product(now[0][...], now[1][...], wh, wl, tile(n))
            if sweep == SWEEPS - 1:
                gh[tile(n), :], gl[tile(n), :] = halves(cf[tile(n), :])
                value = value * math.sqrt(K)
                x[:, tile(n)] = value
            later[0][:, tile(n)], later[1][:, tile(n)] = halves(value)
            yh[tile(n), :], yl[tile(n), :] = halves(value.T)
        now, later = later, now

    my_rows = pl.ds(pl.multiple_of(r * SLAB, SLAB), SLAB)
    iso_ref[...] = x[my_rows, :]

    for n in range(3):
        uh[:, tile(n)], ul[:, tile(n)] = halves(product(yh[my_rows, :], yl[my_rows, :], gh, gl, tile(n)))
    for n in range(3):
        env_ref[:, tile(n)] = product(uh[...], ul[...], now[0], now[1], tile(n))

    for f in range(3):
        gather_sent(f)
    to_owners_sent(c1_send)

    @pl.when(is_owner)
    def _():
        wait(co.at[pl.ds(0, 63)], c2_send)

    wait(cf.at[pl.ds(0, 3 * SLAB)], c3_send)


def hand_on(iso_in, env_in, iso_out, env_out, buf, arrived, left):
    pieces = []
    for n, (src, dst) in enumerate(((iso_in, iso_out), (env_in, env_out))):
        for m in range(2):
            rows = pl.ds(96 * m, 96)
            slot = 2 * n + m
            pieces.append((
                pltpu.make_async_copy(src.at[rows], buf.at[slot], arrived.at[slot]),
                pltpu.make_async_copy(buf.at[slot], dst.at[rows], left.at[slot]),
            ))
    for come, _ in pieces:
        come.start()
    for come, go in pieces:
        come.wait()
        go.start()
    for _, go in pieces:
        go.wait()


def body(amplitudes, left_terms, right_terms, source_list, list_count, weight_index, weight_table):
    vmem = pl.BlockSpec(memory_space=pltpu.VMEM)
    smem = pl.BlockSpec(memory_space=pltpu.SMEM)
    dma = pltpu.SemaphoreType.DMA
    slab = jax.ShapeDtypeStruct((SLAB, K), F32)
    iso, env = pl.pallas_call(
        kernel,
        out_shape=(slab, slab),
        in_specs=[vmem] + [pl.BlockSpec(memory_space=pl.ANY)] * 2 + [smem] * 4,
        out_specs=(vmem, vmem),
        scratch_shapes=[
            pltpu.VMEM((SLAB, K), BF), pltpu.VMEM((SLAB, K), BF),
            *[pltpu.VMEM((K, K), BF)] * 12,
            pltpu.VMEM((SLAB, K), BF), pltpu.VMEM((SLAB, K), BF),
            pltpu.VMEM((SLAB, K), F32),
            pltpu.VMEM((K, K), F32), pltpu.VMEM((K, K), F32), pltpu.VMEM((2, 96, K), F32),
            pltpu.VMEM((3, 2, 16, 6, TR, TC), F32),
            pltpu.VMEM((2, 32, TR, TC), F32),
            pltpu.VMEM((3, TR, TC), F32),
            pltpu.VMEM((64, TR, TC), F32),
            pltpu.VMEM((64, TR, TC), F32),
            pltpu.VMEM((K, K), F32),
            pltpu.VMEM((SLAB, K), F32),
            dma((2,)),
            dma((3,)), dma((3, 6)), dma((3,)), dma((3, 3)), dma((3,)), dma((3, 12)), dma((3,)), dma((3, 16)),
            dma((2,)), dma((2, 3)), dma((2,)), dma((2,)), dma, dma, dma, dma, dma, dma((6,)),
        ],
        compiler_params=pltpu.CompilerParams(
            collective_id=0, has_side_effects=True, vmem_limit_bytes=56 * 1024 * 1024
        ),
        cost_estimate=pl.CostEstimate(flops=28 * 10**9, bytes_accessed=8 * 10**6, transcendentals=0),
    )(
        amplitudes, left_terms.reshape(SLAB, K), right_terms.reshape(K, K),
        source_list.T, list_count, weight_index.T, weight_table,
    )
    anywhere = pl.BlockSpec(memory_space=pl.ANY)
    iso, env = pl.pallas_call(
        hand_on,
        out_shape=(slab, slab),
        in_specs=[anywhere] * 2,
        out_specs=(anywhere,) * 2,
        scratch_shapes=[pltpu.VMEM((4, 96, K), F32), dma((4,)), dma((4,))],
        cost_estimate=pl.CostEstimate(flops=0, bytes_accessed=4 * SLAB * K * 4, transcendentals=0),
    )(iso, env)
    return iso, env.reshape(1, SLAB, K)


def solution(mesh):
    placed = (P("rows", None), P("terms", "rows", None), P("terms", None, None), P(), P(), P(), P())
    return jax.shard_map(
        body,
        mesh=mesh,
        in_specs=placed,
        out_specs=(P("rows", None), P("terms", "rows", None)),
        check_vma=False,
    )
```

```python
import math

import jax
import jax.numpy as jnp
from jax import lax
from jax.experimental import pallas as pl
from jax.experimental.pallas import tpu as pltpu
from jax.sharding import PartitionSpec as P

K = 768
FAN = 4
SWEEPS = 3
SLAB = 192
OWNERS = 48
TR, TC = 8, 384
COEF_ONE = 3.4445
COEF_TWO = -4.775
COEF_THREE = 2.0315
MESH = pl.DeviceIdType.MESH
BF = jnp.bfloat16
F32 = jnp.float32


def halves(value):
    high = value.astype(BF)
    return high, (value - high.astype(F32)).astype(BF)


def split(src, high, low, rows, step):
    @pl.loop(0, rows // step)
    def _(i):
        at = pl.ds(pl.multiple_of(i * step, step), step)
        high[at, :], low[at, :] = halves(src[at, :])


def product(ah, al, bh, bl, cols):
    return joined(ah, al, bh[:, cols], bl[:, cols])


def joined(ah, al, bh, bl):
    rows = ah.shape[0]
    both = jnp.dot(jnp.concatenate([ah, al], axis=0), bh, preferred_element_type=F32)
    return both[:rows] + (both[rows:] + jnp.dot(ah, bl, preferred_element_type=F32))


def wait(ref, sem):
    pltpu.make_async_copy(ref, ref, sem).wait()


def kernel(
    a_ref, l_hbm, r_hbm, source, count, windex, wtable,
    iso_ref, env_ref,
    lh, ll, rh, rl, xh, xl, vh, vl, yh, yl, gh, gl, wh, wl, uh, ul, part, x, w, pre,
    ga, rs, mine, cb, co, cf, l_ref, in_sem,
    z_send, z_recv, s1_send, s1_recv, s2_send, s2_recv, sib_send, sib_recv,
    pre_send, pre_recv, rs_send, rs_recv, c1_send, c1_recv, c2_send, c2_recv, c3_send, c3_recv,
):
    t = lax.axis_index("terms")
    r = lax.axis_index("rows")
    core = t % 2
    cy = (t // 2) % 4
    zl = (t // 8) % 2
    cx = t // 16
    pos = cx * 4 + cy
    dq = zl * 2 + core
    q = jnp.where(pos % 2 == 1, 3 - dq, dq)
    is_owner = q < 3
    own = jnp.minimum(pos * 3 + q, OWNERS - 1)

    def term(xx, zz, yy, cc):
        return ((xx * 2 + zz) * 4 + yy) * 2 + cc

    def owner_term(m):
        p = m // 3
        qq = m % 3
        d = jnp.where(p % 2 == 1, 3 - qq, qq)
        return term(p // 4, d // 2, p % 4, d % 2)

    def chunk(ref, m, row0=0):
        rows = pl.ds(pl.multiple_of(row0 + (m // 2) * TR, TR), TR)
        return ref.at[rows, pl.ds(pl.multiple_of((m % 2) * TC, TC), TC)]

    def there(tt, rr):
        return {"terms": tt, "rows": rr}

    def remote(src, dst, send, recv, tt, rr):
        return pltpu.make_async_remote_copy(
            src_ref=src, dst_ref=dst, send_sem=send, recv_sem=recv,
            device_id=there(tt, rr), device_id_type=MESH,
        )

    bring_l = pltpu.make_async_copy(l_hbm, l_ref, in_sem.at[0])
    bring_r = pltpu.make_async_copy(r_hbm, w, in_sem.at[1])
    bring_l.start()
    bring_r.start()
    barrier = pltpu.get_barrier_semaphore()

    for dr in (2, 1, 3):
        for zz in range(2):
            for cc in range(2):
                pl.semaphore_signal(
                    barrier, inc=1, device_id=there(term(cx, zz, cy, cc), (r + dr) % 4), device_id_type=MESH
                )

    @pl.loop(1, 64)
    def _(i):
        pl.semaphore_signal(barrier, inc=1, device_id=there((t + i) % 64, r), device_id_type=MESH)

    bring_l.wait()
    split(l_ref, lh, ll, SLAB, 48)
    bring_r.wait()
    split(w, rh, rl, K, 64)
    pl.semaphore_wait(barrier, 75)

    def to_owners(src, dst, send, recv):
        @pl.loop(0, OWNERS)
        def _(i):
            m = (i + own) % OWNERS
            o = owner_term(m)
            slot = (t - o + 63) % 64

            @pl.when(o != t)
            def _():
                remote(chunk(src, m), dst.at[slot], send, recv, o, r).start()

        @pl.when(is_owner)
        def _():
            dst[63] = chunk(src, own)[...]

    def to_owners_sent(send):
        @pl.when(is_owner)
        def _():
            wait(cb.at[pl.ds(0, 47)], send)

        @pl.when(jnp.logical_not(is_owner))
        def _():
            wait(cb.at[pl.ds(0, 48)], send)

    sibling = term(cx, zl, cy, 1 - core)
    kept = pl.ds(pl.multiple_of(core * 96, 96), 96)
    given = pl.ds(pl.multiple_of((1 - core) * 96, 96), 96)
    keeps_own = jnp.logical_and(is_owner, own // 24 == core)

    def tile(n):
        return pl.ds(n * 256, 256)

    def pre_start(f, n):
        remote(part.at[given, tile(n)], pre.at[f, :, tile(n)], pre_send.at[f], pre_recv.at[f, n], sibling, r).start()

    def pre_add(f, n):
        wait(pre.at[f, :, tile(n)], pre_recv.at[f, n])
        part[kept, tile(n)] = part[kept, tile(n)] + pre[f, :, tile(n)]

    def reduce_start(f, side):
        @pl.loop(0, 12)
        def _(i):
            m = 24 * core + 2 * ((i + pos) % 12) + side
            o = owner_term(m)
            dst = rs.at[f, (t // 2 - o // 2 + 31) % 32]

            @pl.when(o != t)
            def _():
                remote(chunk(part, m), dst, rs_send.at[f], rs_recv.at[f], o, r).start()

            @pl.when(o == t)
            def _():
                pltpu.make_async_copy(chunk(part, m), dst, rs_recv.at[f]).start()

    def reduce_sent(f):
        wait(pre.at[f], pre_send.at[f])

        @pl.when(keeps_own)
        def _():
            wait(rs.at[f, pl.ds(0, 23)], rs_send.at[f])

        @pl.when(jnp.logical_not(keeps_own))
        def _():
            wait(rs.at[f, pl.ds(0, 24)], rs_send.at[f])

    side_b = jnp.where(core == 0, cx, cy)
    side_a = jnp.where(core == 0, cy, cx)
    here = side_b * 4 + side_a
    kk = 4 * jnp.minimum(q, 2) + r
    to_core = kk // 6
    to_slot = kk % 6
    to_pos = jnp.where(to_core == 0, cx * 4 + cy, cy * 4 + cx)

    def partner(bb, aa):
        return term(jnp.where(core == 0, bb, aa), zl, jnp.where(core == 0, aa, bb), core)

    def gather_start(f):
        @pl.when(is_owner)
        def _():
            for dr in (2, 1, 3, 0):
                for dz in (1, 0):
                    tt, rr = term(cx, (zl + dz) % 2, cy, to_core), (r + dr) % 4
                    dst = ga.at[f, to_core, to_pos, to_slot]
                    if dz == 0 and dr == 0:
                        @pl.when(to_core == core)
                        def _():
                            pltpu.make_async_copy(mine.at[f], dst, z_recv.at[f, to_slot]).start()

                        @pl.when(to_core != core)
                        def _():
                            remote(mine.at[f], dst, z_send.at[f], z_recv.at[f, to_slot], tt, rr).start()
                    else:
                        remote(mine.at[f], dst, z_send.at[f], z_recv.at[f, to_slot], tt, rr).start()

    def gather_rest(f, after_z=None, after_push=None):
        for i in range(6):
            wait(ga.at[f, core, here, i], z_recv.at[f, i])

        def block(bb, d):
            return ga.at[f, core, bb * 4 + (side_a + 4 - d) % 4]

        def across(bb, d, sem):
            remote(block(bb, d), block(bb, d), sib_send.at[f], sib_recv.at[f, sem], sibling, r).start()

        def push(bb, d, tt, sem):
            remote(block(bb, d), block(bb, d), s2_send.at[f], s2_recv.at[f, sem], tt, r).start()

        mine_now = block(side_b, 0)
        for d in (1, 3, 2):
            remote(mine_now, mine_now, s1_send.at[f], s1_recv.at[f, d - 1], partner(side_b, (side_a + d) % 4), r).start()
        if after_z:
            after_z()
        order = (0, 1, 3, 2)
        for d in order:
            if d > 0:
                wait(block(side_b, d), s1_recv.at[f, d - 1])
            for n in (1, 3):
                push(side_b, d, partner((side_b + n) % 4, side_a), 4 * (n - 1) + d)
            across(side_b, d, d)
        if after_push:
            after_push()
        for n, d in [(n, d) for d in order for n in (1, 3)] + [(2, d) for d in (0, 1, 3, 2)]:
            bb = (side_b + 4 - n) % 4
            wait(block(bb, d), s2_recv.at[f, 4 * (n - 1) + d])
            if (n, d) in ((1, 0), (3, 1), (1, 3), (3, 2)):
                push(bb, d, partner((side_b + n) % 4, side_a), 4 + d)
            across(bb, d, 4 * n + d)
        for n in (0, 1, 3, 2):
            for d in order:
                bb = (side_a + 4 - n) % 4
                wait(ga.at[f, 1 - core, bb * 4 + (side_b + 4 - d) % 4], sib_recv.at[f, 4 * n + d])

    def gather_sent(f):
        @pl.when(is_owner)
        def _():
            @pl.when(to_core == core)
            def _():
                wait(cb.at[pl.ds(0, 7)], z_send.at[f])

            @pl.when(to_core != core)
            def _():
                wait(cb.at[pl.ds(0, 8)], z_send.at[f])

        wait(ga.at[f, 0, pl.ds(0, 3)], s1_send.at[f])
        wait(ga.at[f, 0, pl.ds(0, 12)], s2_send.at[f])
        wait(ga.at[f, 0], sib_send.at[f])

    def assemble(f):
        for cc in range(2):
            @pl.loop(0, 16)
            def _(s):
                p = s if cc == 0 else (s % 4) * 4 + s // 4
                for i in range(6):
                    k = 6 * cc + i
                    m = p * 3 + k // 4
                    chunk(x, m, (k % 4) * SLAB)[...] = ga[f, cc, s, i]

    def apply_terms(f):
        for n in range(3):
            high, low = halves(x[:, tile(n)])
            uh[:, tile(n)], ul[:, tile(n)] = halves(joined(lh[...], ll[...], high, low))

        for n in range(3):
            part[:, tile(n)] = product(uh[...], ul[...], rh, rl, tile(n))
            pre_start(f, n)
        pre_add(f, 0)
        pre_add(f, 1)
        reduce_start(f, 0)
        pre_add(f, 2)
        reduce_start(f, 1)

    @pl.when(is_owner)
    def _():
        mine[0] = chunk(a_ref, own)[...]

    gather_start(0)
    to_owners(l_ref, cb, c1_send, c1_recv)
    gather_rest(0)

    ring_right, ring_left, ring_far = (r + 1) % 4, (r + 3) % 4, (r + 2) % 4

    def slab_half(rr, hh):
        return cf.at[pl.ds(pl.multiple_of(rr * SLAB + hh * 96, 96), 96)]

    def go_round(rr, hh, to, sem):
        remote(slab_half(rr, hh), slab_half(rr, hh), c3_send, c3_recv.at[sem], t, to).start()

    def mix():
        @pl.when(is_owner)
        def _():
            wait(cb.at[pl.ds(0, 63)], c1_recv)

            @pl.loop(0, 64)
            def _(j):
                total = jnp.zeros((TR, TC), F32)
                for c in range(FAN):
                    weight = jnp.where(c < count[j], wtable[windex[c, j]], 0.0)
                    total = total + weight * cb[(source[c, j] - t + 63) % 64]
                co[j] = total

    def give_back():
        @pl.when(is_owner)
        def _():
            dst = chunk(cf, own, r * SLAB)

            @pl.loop(1, 64)
            def _(i):
                j = (i + t) % 64
                remote(co.at[j], dst, c2_send, c2_recv, j, r).start()

            pltpu.make_async_copy(co.at[t], dst, c2_recv).start()

    def first_round():
        wait(cf.at[pl.ds(pl.multiple_of(r * SLAB, SLAB), SLAB)], c2_recv)
        go_round(r, 0, ring_right, 0)
        go_round(r, 1, ring_left, 2)

    def second_round():
        go_round(r, 1, ring_right, 1)
        go_round(r, 0, ring_left, 3)
        wait(slab_half(ring_left, 0), c3_recv.at[0])
        go_round(ring_left, 0, ring_right, 4)
        wait(slab_half(ring_right, 1), c3_recv.at[2])
        go_round(ring_right, 1, ring_left, 5)

    for f in range(2):
        assemble(f)
        apply_terms(f)
        if f == 0:
            mix()

        @pl.when(is_owner)
        def _():
            wait(rs.at[f], rs_recv.at[f])
            mine[f + 1] = mine[f] - 0.3 * jnp.sum(rs[f], axis=0)

        gather_start(f + 1)
        if f == 0:
            give_back()
        reduce_sent(f)
        if f == 0:
            gather_rest(1, after_push=first_round)
        else:
            gather_rest(2, after_z=second_round)

    assemble(2)
    squares = jnp.sum(lax.fori_loop(
        0, 12,
        lambda i, s: s + jnp.sum((x[pl.ds(pl.multiple_of(i * 64, 64), 64), :] ** 2).reshape(8, 8, K), axis=0),
        jnp.zeros((8, K), F32),
    ))
    scale = 1.0 / jnp.sqrt(jnp.full((8, 128), squares, F32))[0:1, 0:1]
    for n in range(3):
        value = x[tile(n), :] * scale
        xh[tile(n), :], xl[tile(n), :] = halves(value)
        yh[:, tile(n)], yl[:, tile(n)] = halves(value.T)

    def symmetric(ah, al, bh, bl, oh, ol, last):
        for n in range(3):
            top = 256 * (n + 1)
            value = last(product(ah[:top, :], al[:top, :], bh, bl, tile(n)), n)
            oh[:top, tile(n)], ol[:top, tile(n)] = halves(value)
            for m in range(n):
                oh[tile(n), tile(m)], ol[tile(n), tile(m)] = halves(value[256 * m:256 * (m + 1)].T)

    def polynomial(value, n):
        top = value.shape[0]
        gram = gh[:top, tile(n)].astype(F32) + gl[:top, tile(n)].astype(F32)
        row = lax.broadcasted_iota(jnp.int32, value.shape, 0)
        col = lax.broadcasted_iota(jnp.int32, value.shape, 1) + 256 * n
        return COEF_TWO * gram + COEF_THREE * value + jnp.where(row == col, COEF_ONE, 0.0)

    now, later = (xh, xl), (vh, vl)
    for sweep in range(SWEEPS):
        symmetric(yh, yl, now[0], now[1], gh, gl, lambda value, n: value)
        symmetric(gh, gl, gh, gl, wh, wl, polynomial)
        if sweep == SWEEPS - 1:
            for rr, hh, sem in ((ring_left, 1, 1), (ring_right, 0, 3), (ring_far, 0, 4), (ring_far, 1, 5)):
                wait(slab_half(rr, hh), c3_recv.at[sem])
        for n in range(3):
            value = product(now[0][...], now[1][...], wh, wl, tile(n))
            if sweep == SWEEPS - 1:
                gh[tile(n), :], gl[tile(n), :] = halves(cf[tile(n), :])
                value = value * math.sqrt(K)
                x[:, tile(n)] = value
            later[0][:, tile(n)], later[1][:, tile(n)] = halves(value)
            yh[tile(n), :], yl[tile(n), :] = halves(value.T)
        now, later = later, now

    my_rows = pl.ds(pl.multiple_of(r * SLAB, SLAB), SLAB)
    iso_ref[...] = x[my_rows, :]

    for n in range(3):
        uh[:, tile(n)], ul[:, tile(n)] = halves(product(yh[my_rows, :], yl[my_rows, :], gh, gl, tile(n)))
    for n in range(3):
        env_ref[:, tile(n)] = product(uh[...], ul[...], now[0], now[1], tile(n))

    for f in range(3):
        gather_sent(f)
    to_owners_sent(c1_send)

    @pl.when(is_owner)
    def _():
        wait(co.at[pl.ds(0, 63)], c2_send)

    wait(cf.at[pl.ds(0, 3 * SLAB)], c3_send)


def hand_on(iso_in, env_in, iso_out, env_out, buf, arrived, left):
    pieces = []
    for n, (src, dst) in enumerate(((iso_in, iso_out), (env_in, env_out))):
        for m in range(2):
            rows = pl.ds(96 * m, 96)
            slot = 2 * n + m
            pieces.append((
                pltpu.make_async_copy(src.at[rows], buf.at[slot], arrived.at[slot]),
                pltpu.make_async_copy(buf.at[slot], dst.at[rows], left.at[slot]),
            ))
    for come, _ in pieces:
        come.start()
    for come, go in pieces:
        come.wait()
        go.start()
    for _, go in pieces:
        go.wait()


def body(amplitudes, left_terms, right_terms, source_list, list_count, weight_index, weight_table):
    vmem = pl.BlockSpec(memory_space=pltpu.VMEM)
    smem = pl.BlockSpec(memory_space=pltpu.SMEM)
    dma = pltpu.SemaphoreType.DMA
    slab = jax.ShapeDtypeStruct((SLAB, K), F32)
    iso, env = pl.pallas_call(
        kernel,
        out_shape=(slab, slab),
        in_specs=[vmem] + [pl.BlockSpec(memory_space=pl.ANY)] * 2 + [smem] * 4,
        out_specs=(vmem, vmem),
        scratch_shapes=[
            pltpu.VMEM((SLAB, K), BF), pltpu.VMEM((SLAB, K), BF),
            *[pltpu.VMEM((K, K), BF)] * 12,
            pltpu.VMEM((SLAB, K), BF), pltpu.VMEM((SLAB, K), BF),
            pltpu.VMEM((SLAB, K), F32),
            pltpu.VMEM((K, K), F32), pltpu.VMEM((K, K), F32), pltpu.VMEM((2, 96, K), F32),
            pltpu.VMEM((3, 2, 16, 6, TR, TC), F32),
            pltpu.VMEM((2, 32, TR, TC), F32),
            pltpu.VMEM((3, TR, TC), F32),
            pltpu.VMEM((64, TR, TC), F32),
            pltpu.VMEM((64, TR, TC), F32),
            pltpu.VMEM((K, K), F32),
            pltpu.VMEM((SLAB, K), F32),
            dma((2,)),
            dma((3,)), dma((3, 6)), dma((3,)), dma((3, 3)), dma((3,)), dma((3, 12)), dma((3,)), dma((3, 16)),
            dma((2,)), dma((2, 3)), dma((2,)), dma((2,)), dma, dma, dma, dma, dma, dma((6,)),
        ],
        compiler_params=pltpu.CompilerParams(
            collective_id=0, has_side_effects=True, vmem_limit_bytes=56 * 1024 * 1024
        ),
        cost_estimate=pl.CostEstimate(flops=28 * 10**9, bytes_accessed=8 * 10**6, transcendentals=0),
    )(
        amplitudes, left_terms.reshape(SLAB, K), right_terms.reshape(K, K),
        source_list.T, list_count, weight_index.T, weight_table,
    )
    anywhere = pl.BlockSpec(memory_space=pl.ANY)
    iso, env = pl.pallas_call(
        hand_on,
        out_shape=(slab, slab),
        in_specs=[anywhere] * 2,
        out_specs=(anywhere,) * 2,
        scratch_shapes=[pltpu.VMEM((4, 96, K), F32), dma((4,)), dma((4,))],
        cost_estimate=pl.CostEstimate(flops=0, bytes_accessed=4 * SLAB * K * 4, transcendentals=0),
    )(iso, env)
    return iso, env.reshape(1, SLAB, K)


def solution(mesh):
    placed = (P("rows", None), P("terms", "rows", None), P("terms", None, None), P(), P(), P(), P())
    return jax.shard_map(
        body,
        mesh=mesh,
        in_specs=placed,
        out_specs=(P("rows", None), P("terms", "rows", None)),
        check_vma=False,
    )
```
